256 devices in a mesh: store: 64 (over x, z, core), grp: 4 (over y).
Axes of the slice: x: 4, y: 4, z: 8, core: 2. Of those that a mesh axis runs over, the one named last changes fastest.
Arguments:
- embeddings: float32 [2048, 512, 512], P(('store', 'grp'))
- cluster_ids: int32 [2048, 512], P(('store', 'grp')), may hold values from 0 to 31
- block_slot: int32 [512], replicated, may hold values from 0 to 511, each once
- pairs: int32 [512, 2], P(('store', 'grp')), may hold values from 0 to 511, as said below
Outputs:
- best_cosine: float32 [2048, 512], P(('store', 'grp'))
The draws below stay inside these ranges and needn't reach their ends.
Inputs may be any that keep to these rules, and one draw needn't show every extreme that they name: `pairs`: block numbers; in every pair the first block number is at most the second.
All inputs are finite; a program needn't handle non-finite values.
Results may differ from the reference program's by a relative error of at most 0.00052.
Values may be sent and summed in bfloat16 or wider, within the bound.
A program may use at most 128 MiB of HBM per device.

```python
import jax
import jax.numpy as jnp
from jax import lax

D = 512
BLK = 2048
NCL = 32
NB = 512
PAIRS = 512


def block_clusters(key):
    cuts = jax.random.permutation(key, NB - 1)[:NCL - 1] + 1
    blocks = jnp.arange(NB)
    return jnp.sum((cuts[None, :] <= blocks[:, None]).astype(jnp.int32), axis=1).astype(jnp.int32)


def draw_embeddings(key, part):
    key = jax.random.fold_in(key, 5)
    keys = jax.random.split(key, 3)
    base = jax.random.normal(keys[0], (BLK, NB, D), jnp.float32)
    mixed = base + 0.7 * jnp.roll(jnp.roll(base, BLK // 2, 0), 1, 1)
    row_scale = jnp.exp(jax.random.uniform(keys[1], (BLK, NB, 1), jnp.float32, 0.0, 2.3))
    col_scale = jnp.exp(jax.random.uniform(keys[2], (1, 1, D), jnp.float32, 0.0, 2.3))
    return mixed * row_scale * col_scale


def draw_cluster_ids(key, part):
    owner = block_clusters(key)
    key = jax.random.fold_in(key, 11)
    keys = jax.random.split(key, 2)
    noisy = jax.random.randint(keys[0], (BLK, NB), 0, 4) == 0
    other = jax.random.randint(keys[1], (BLK, NB), 0, NCL)
    return jnp.where(noisy, other, owner[None, :]).astype(jnp.int32)


def draw_pairs(key, part):
    owner = block_clusters(key)
    key = jax.random.fold_in(key, 17)
    keys = jax.random.split(key, 2)
    ends = jnp.sum((owner[None, :] <= owner[:, None]).astype(jnp.int32), axis=1)
    first = jax.random.randint(keys[0], (PAIRS,), 0, NB)
    first = first.at[0].set(NB - 1)
    first = first.at[1].set(0)
    span = jnp.take(ends, first) - first
    second = first + jax.random.randint(keys[1], (PAIRS,), 0, 1 << 20) % span
    return jnp.stack([first, second], axis=1).astype(jnp.int32)


def setup_inputs(seed: int = 0) -> dict:
    streams_of = jax.random.split(jax.random.key(seed), 5)
    return {
        "embeddings": draw_embeddings(jax.random.fold_in(streams_of[4], 71), 0),
        "cluster_ids": draw_cluster_ids(jax.random.fold_in(streams_of[4], 71), 0),
        "block_slot": jax.random.permutation(streams_of[2], NB).astype(jnp.int32),
        "pairs": draw_pairs(jax.random.fold_in(streams_of[4], 71), 0),
    }


def unit_block(embeddings, cluster_ids, block_slot, block):
    slot = jnp.take(block_slot, block).astype(jnp.int32)
    rows = lax.dynamic_index_in_dim(embeddings, slot, 1, keepdims=False)
    norms = lax.rsqrt(lax.optimization_barrier(jnp.sum(rows * rows, axis=-1, keepdims=True)) + jnp.float32(1e-06))
    ids = lax.dynamic_index_in_dim(cluster_ids, slot, 1, keepdims=False)
    return ((rows * norms).astype(jnp.bfloat16), ids)

def reference(embeddings, cluster_ids, block_slot, pairs):
    count = embeddings.shape[1]
    length = embeddings.shape[0]
    diagonal = jnp.arange(length)[:, None] == jnp.arange(length)[None, :]

    def one_pair(best, pair):
        first, second = (pair[0], pair[1])
        left, left_ids = unit_block(embeddings, cluster_ids, block_slot, first)
        right, right_ids = unit_block(embeddings, cluster_ids, block_slot, second)
        gram = jnp.dot(left, right.T, preferred_element_type=jnp.float32)
        keep = (left_ids[:, None] == right_ids[None, :]) & jnp.logical_not((first == second) & diagonal)
        masked = jnp.where(keep, gram, jnp.float32(-1.0))
        best = best.at[first].max(lax.optimization_barrier(jnp.max(masked, axis=1)))
        best = best.at[second].max(lax.optimization_barrier(jnp.max(masked, axis=0)))
        return (best, None)
    start = jnp.full((count, length), -1.0, jnp.float32)
    best, unused = lax.scan(one_pair, start, pairs)
    return jnp.zeros((length, count), jnp.float32).at[:, block_slot].set(best.T)
```

```python
import functools

import jax
import jax.numpy as jnp
from jax import lax
from jax.experimental import pallas as pl
from jax.experimental.pallas import tpu as pltpu
from jax.sharding import PartitionSpec as P

MESH = pl.DeviceIdType.MESH
NZ, NXY, NC = 8, 16, 2
KCHIP = 6
EDGES = 6
KPLANE = 64
SETS = NZ * NXY
ROWS = 8


def pair_maxima(left, right, left_ids, right_ids, same):
    length = left.shape[0]
    step_rows = min(512, length)
    columns = jnp.arange(length)

    def row_block(start):
        piece = lax.dynamic_slice_in_dim(left, start, step_rows, 0)
        piece_ids = lax.dynamic_slice_in_dim(left_ids, start, step_rows, 0)
        gram = lax.dot_general(
            piece, right, (((1,), (1,)), ((), ())), preferred_element_type=jnp.float32
        )
        rows = start + jnp.arange(step_rows)
        keep = (piece_ids[:, None] == right_ids[None, :]) & jnp.logical_not(
            same & (rows[:, None] == columns[None, :])
        )
        masked = jnp.where(keep, gram, jnp.float32(-1.0))
        return (jnp.max(masked, axis=1), jnp.max(masked, axis=0))

    starts = jnp.arange(length // step_rows) * step_rows
    row_best, col_best = lax.map(row_block, starts)
    return (row_best.reshape(length), jnp.max(col_best, axis=0))


def any_pairs(embeddings, cluster_ids, block_slot, every_need, needed):
    tile_rows, count, width = embeddings.shape
    n_store = lax.axis_size("store")
    n_grp = lax.axis_size("grp")
    length = tile_rows * n_store * n_grp
    norms = lax.rsqrt(jnp.sum(embeddings * embeddings, axis=-1, keepdims=True) + jnp.float32(1e-06))
    unit = jnp.transpose((embeddings * norms).astype(jnp.bfloat16), (1, 0, 2))
    ids_by_slot = cluster_ids.T
    slots_needed = needed.shape[0]
    asked = jnp.transpose(every_need.reshape(n_store, n_grp, slots_needed), (2, 0, 1))
    asked_slots = jnp.take(block_slot, asked)
    send_rows = jnp.take(unit, asked_slots, axis=0)
    send_ids = jnp.take(ids_by_slot, asked_slots, axis=0)

    def exchange(rows):
        rows = lax.all_to_all(rows, "store", split_axis=1, concat_axis=1, tiled=True)
        return lax.all_to_all(rows, "grp", split_axis=2, concat_axis=2, tiled=True)

    blocks = exchange(send_rows).reshape(slots_needed, length, width)
    block_ids = exchange(send_ids).reshape(slots_needed, length)
    results = []
    for index in range(slots_needed // 2):
        same = needed[2 * index] == needed[2 * index + 1]
        results += pair_maxima(
            blocks[2 * index], blocks[2 * index + 1], block_ids[2 * index], block_ids[2 * index + 1], same
        )
    maxima = jnp.stack(results, axis=0)
    table = jnp.full((count, length), -1.0, jnp.float32).at[needed].max(maxima)
    table = lax.pmax(table, ("store", "grp"))
    position = lax.axis_index(("store", "grp"))
    mine = lax.dynamic_slice_in_dim(table, position * tile_rows, tile_rows, 1)
    return jnp.zeros((tile_rows, count), jnp.float32).at[:, block_slot].set(mine.T)


def chain_kernel(next_ref, table_ref, out_ref, end_ref):
    def step(t, s):
        out_ref[pl.ds(t, 1), :] = table_ref[pl.ds(s, 1), :]
        return next_ref[s]

    end_ref[0] = lax.fori_loop(0, SETS, step, jnp.int32(0))


def chip_sets(first, second):
    n = first.shape[0]
    order = jnp.arange(n)
    key = (second * n + first) * n + order
    rank = jnp.sum((key[None, :] < key[:, None]).astype(jnp.int32), axis=1)
    hot = rank[None, :] == order[:, None]
    a = jnp.sum(jnp.where(hot, first[None, :], 0), axis=1)
    b = jnp.sum(jnp.where(hot, second[None, :], 0), axis=1)
    nodes = [jnp.full((n,), -1, jnp.int32)] * KCHIP
    count = jnp.zeros((n,), jnp.int32)
    alive = jnp.ones((n,), bool)
    length = jnp.zeros((n,), jnp.int32)
    left_at, right_at = [], []
    for w in range(EDGES):
        aw = jnp.concatenate([a[w:], jnp.full((w,), -2, jnp.int32)])
        bw = jnp.concatenate([b[w:], jnp.full((w,), -2, jnp.int32)])
        at_a = functools.reduce(jnp.maximum, [jnp.where(v == aw, m, -1) for m, v in enumerate(nodes)])
        at_b = functools.reduce(jnp.maximum, [jnp.where(v == bw, m, -1) for m, v in enumerate(nodes)])
        new_a = at_a < 0
        new_b = (at_b < 0) & (aw != bw)
        la = jnp.where(new_a, count, at_a)
        after = count + new_a.astype(jnp.int32)
        lb = jnp.where(aw == bw, la, jnp.where(new_b, after, at_b))
        total = after + new_b.astype(jnp.int32)
        alive = alive & (total <= KCHIP) & (order + w < n)
        nodes = [
            jnp.where(alive & new_a & (la == m), aw, jnp.where(alive & new_b & (lb == m), bw, v))
            for m, v in enumerate(nodes)
        ]
        count = jnp.where(alive, total, count)
        length = length + alive.astype(jnp.int32)
        left_at.append(la)
        right_at.append(lb)
    zero = jnp.zeros((n,), jnp.int32)
    pad = [zero, zero]
    table = jnp.stack(nodes + pad + left_at + pad + right_at + pad + [length], axis=1)
    blank = jnp.array([[-1] * KCHIP + [0] * 19], jnp.int32)
    table = jnp.concatenate([table, jnp.tile(blank, (8, 1))], axis=0)
    table = jnp.pad(table, ((0, 0), (0, 128 - table.shape[1])))
    following = jnp.concatenate([order + length, jnp.full((8,), n, jnp.int32)]).astype(jnp.int32)
    sets, end = pl.pallas_call(
        chain_kernel,
        out_shape=(jax.ShapeDtypeStruct((SETS, 128), jnp.int32), jax.ShapeDtypeStruct((1,), jnp.int32)),
        in_specs=[pl.BlockSpec(memory_space=pltpu.SMEM), pl.BlockSpec(memory_space=pltpu.VMEM)],
        out_specs=(pl.BlockSpec(memory_space=pltpu.VMEM), pl.BlockSpec(memory_space=pltpu.SMEM)),
    )(following, table)
    return sets, end[0] == n


def plane_sets(sets):
    t = jnp.arange(SETS)
    node = sets[:, :KCHIP]
    flat = node.reshape(-1)
    set_of = jnp.repeat(t, KCHIP)
    earlier = (flat[None, :] == flat[:, None]) & (set_of[None, :] < set_of[:, None])
    prev = jnp.max(jnp.where(earlier, set_of[None, :], -1), axis=1)
    valid = flat >= 0
    fresh = (prev[None, :] < t[:, None]) & valid[None, :] & (set_of[None, :] >= t[:, None])
    upto = (set_of[:, None] <= t[None, :]).astype(jnp.bfloat16)
    distinct = jnp.dot(fresh.astype(jnp.bfloat16), upto, preferred_element_type=jnp.float32)
    fits = (t[None, :] >= t[:, None]) & (t[None, :] < t[:, None] + NXY) & (distinct <= KPLANE)
    following = t + jnp.sum(fits.astype(jnp.int32), axis=1)
    starts = [jnp.int32(0)]
    for _ in range(NZ):
        here = jnp.sum(jnp.where(t == starts[-1], following, 0))
        starts.append(jnp.where(starts[-1] >= SETS, SETS, here))
    fits_all = starts[NZ] >= jnp.sum((sets[:, 24] > 0).astype(jnp.int32))
    begin = jnp.stack(starts[:NZ])
    end = jnp.stack(starts[1:])
    at = begin[:, None] + jnp.arange(NXY)[None, :]
    held = at < end[:, None]
    chips = jnp.take(sets, jnp.minimum(at, SETS - 1).reshape(-1), axis=0).reshape(NZ, NXY, 128)
    entry = jnp.where(held[:, :, None], chips[:, :, :KCHIP], -1).reshape(NZ, NXY * KCHIP)
    edge_count = jnp.where(held, chips[:, :, 24], 0)
    m = jnp.arange(NXY * KCHIP)
    equal = entry[:, :, None] == entry[:, None, :]
    first = (entry >= 0) & jnp.logical_not(jnp.any(equal & (m[None, None, :] < m[None, :, None]), axis=2))
    position = jnp.sum((first[:, None, :] & (m[None, None, :] < m[None, :, None])).astype(jnp.int32), axis=2)
    local = jnp.sum(jnp.where(equal & first[:, None, :], position[:, None, :], 0), axis=2)
    local = jnp.where(entry >= 0, local, 0)
    k = jnp.arange(KPLANE)
    plane_nodes = jnp.sum(
        jnp.where(first[:, None, :] & (position[:, None, :] == k[None, :, None]), entry[:, None, :], 0), axis=2
    )
    return plane_nodes, local, entry, chips, edge_count, fits_all


def pack(embeddings, slots):
    return pl.pallas_call(
        pack_rows_kernel,
        grid_spec=pltpu.PrefetchScalarGridSpec(
            num_scalar_prefetch=1,
            grid=(NZ,),
            in_specs=[pl.BlockSpec(memory_space=pl.ANY)],
            out_specs=pl.BlockSpec((1, KPLANE, ROWS, 512), lambda p, s: (p, 0, 0, 0)),
            scratch_shapes=[
                pltpu.VMEM((2, KPLANE, ROWS, 512), jnp.float32),
                pltpu.SemaphoreType.DMA((2,)),
            ],
        ),
        out_shape=jax.ShapeDtypeStruct((NZ, KPLANE, ROWS, 512), jnp.bfloat16),
        compiler_params=pltpu.CompilerParams(
            dimension_semantics=("arbitrary",), vmem_limit_bytes=32 << 20
        ),
    )(slots, embeddings)


def pack_rows_kernel(slot_ref, emb_ref, out_ref, raw, sems):
    plane = pl.program_id(0)
    planes = pl.num_programs(0)

    def fetch(p, buf):
        def one(n, carry):
            pltpu.make_async_copy(
                emb_ref.at[:, slot_ref[p * KPLANE + n], :], raw.at[buf, n], sems.at[buf]
            ).start()
            return carry

        lax.fori_loop(0, KPLANE, one, 0)

    @pl.when(plane == 0)
    def _():
        fetch(0, 0)

    buf = lax.rem(plane, 2)

    @pl.when(plane + 1 < planes)
    def _():
        fetch(plane + 1, 1 - buf)

    pltpu.make_async_copy(raw.at[buf], raw.at[buf], sems.at[buf]).wait()

    def norm(n, carry):
        rows = raw[buf, pl.ds(n * 8, 8)]
        scale = lax.rsqrt(jnp.sum(rows * rows, axis=-1, keepdims=True) + jnp.float32(1e-06))
        out_ref[0, pl.ds(n * 8, 8)] = (rows * scale).astype(jnp.bfloat16)
        return carry

    lax.fori_loop(0, KPLANE // 8, norm, 0)


Z_ORDER = (1, 7, 2, 6, 3, 5, 4)


def spread_kernel(sel_ref, rows_ref, ids_ref, out_ref, idout_ref, *scratch):
    land = scratch[:7]
    idland = scratch[7:14]
    pick, zsend, zrecv, psend, precv, csend, crecv, isend, irecv, jsend, jrecv, local_sem, bsend, brecv = scratch[14:]
    store, y = lax.axis_index("store"), lax.axis_index("grp")
    x, z, c = store // 16, (store // 2) % 8, store % 2

    def device(dx, dy, dz, dc):
        return ((((x + dx) % 4) * 8 + (z + dz) % 8) * 2 + (c + dc) % 2, (y + dy) % 4)

    peers = [device(0, 0, dz, 0) for dz in range(1, 8)]
    peers += [device(dx, dy, 0, 0) for dx in range(4) for dy in range(4) if (dx, dy) != (0, 0)]
    peers += [device(0, 0, 0, 1)]
    barrier = pltpu.get_barrier_semaphore()
    for peer in peers:
        pl.semaphore_signal(barrier, inc=1, device_id=peer, device_id_type=MESH)
    pl.semaphore_wait(barrier, len(peers))

    z_copies = {}
    for dz in Z_ORDER:
        rows = pltpu.make_async_remote_copy(
            src_ref=rows_ref.at[(z + dz) % 8], dst_ref=land[dz - 1],
            send_sem=zsend.at[dz], recv_sem=zrecv.at[dz],
            device_id=device(0, 0, dz, 0), device_id_type=MESH,
        )
        ids = pltpu.make_async_remote_copy(
            src_ref=ids_ref.at[(z + dz) % 8], dst_ref=idland[dz - 1],
            send_sem=isend.at[dz], recv_sem=irecv.at[dz],
            device_id=device(0, 0, dz, 0), device_id_type=MESH,
        )
        ids.start()
        rows.start()
        z_copies[dz] = (rows, ids)

    p_copies = {}
    c_copies = {}
    l_copies = {}

    def plane_send(dz):
        if dz == 0:
            def chip(q, carry):
                for n in range(KCHIP):
                    pick[0, q, n] = rows_ref[z, sel_ref[q * KCHIP + n]]
                return carry
            id_src = ids_ref.at[z]
        else:
            rows, ids = z_copies[dz]
            rows.wait_recv()
            ids.wait_recv()

            def chip(q, carry):
                for n in range(KCHIP):
                    pick[dz, q, n] = land[dz - 1][sel_ref[q * KCHIP + n]]
                return carry
            id_src = idland[dz - 1]
        lax.fori_loop(0, NXY, chip, 0)
        copies = []
        for dx in range(4):
            for dy in range(4):
                d = dx * 4 + dy
                q = ((x + dx) % 4) * 4 + (y + dy) % 4
                if d == 0:
                    one = pltpu.make_async_copy(pick.at[dz, q], out_ref.at[0, :, dz, 0], local_sem.at[dz, 0])
                    two = pltpu.make_async_copy(id_src, idout_ref.at[0, dz, 0], local_sem.at[dz, 1])
                    one.start()
                    two.start()
                    l_copies[dz] = (one, two)
                    continue
                one = pltpu.make_async_remote_copy(
                    src_ref=pick.at[dz, q], dst_ref=out_ref.at[0, :, dz, d],
                    send_sem=psend.at[dz, d], recv_sem=precv.at[dz, d],
                    device_id=device(dx, dy, 0, 0), device_id_type=MESH,
                )
                two = pltpu.make_async_remote_copy(
                    src_ref=id_src, dst_ref=idout_ref.at[0, dz, d],
                    send_sem=jsend.at[dz, d], recv_sem=jrecv.at[dz, d],
                    device_id=device(dx, dy, 0, 0), device_id_type=MESH,
                )
                two.start()
                one.start()
                copies += [one, two]
        p_copies[dz] = copies

    def core_send(dz):
        for copy in p_copies[dz]:
            copy.wait_recv()
        for copy in l_copies[dz]:
            copy.wait()
        one = pltpu.make_async_remote_copy(
            src_ref=out_ref.at[0, :, dz], dst_ref=out_ref.at[1, :, dz],
            send_sem=csend.at[dz], recv_sem=crecv.at[dz],
            device_id=device(0, 0, 0, 1), device_id_type=MESH,
        )
        two = pltpu.make_async_remote_copy(
            src_ref=idout_ref.at[0, dz], dst_ref=idout_ref.at[1, dz],
            send_sem=bsend.at[dz], recv_sem=brecv.at[dz],
            device_id=device(0, 0, 0, 1), device_id_type=MESH,
        )
        one.start()
        two.start()
        c_copies[dz] = (one, two)

    order = (0,) + Z_ORDER
    for i, dz in enumerate(order):
        plane_send(dz)
        if i >= 2:
            core_send(order[i - 2])
    core_send(order[-2])
    core_send(order[-1])
    for dz in order:
        for copy in c_copies[dz]:
            copy.wait()
        for copy in p_copies[dz]:
            copy.wait_send()
        if dz:
            for copy in z_copies[dz]:
                copy.wait_send()


def spread(sel, rows, ids):
    dma = pltpu.SemaphoreType.DMA
    return pl.pallas_call(
        spread_kernel,
        out_shape=(
            jax.ShapeDtypeStruct((NC, KCHIP, NZ, NXY, ROWS, 512), jnp.bfloat16),
            jax.ShapeDtypeStruct((NC, NZ, NXY, ROWS, 128), jnp.bfloat16),
        ),
        in_specs=[
            pl.BlockSpec(memory_space=pltpu.SMEM),
            pl.BlockSpec(memory_space=pltpu.VMEM),
            pl.BlockSpec(memory_space=pltpu.VMEM),
        ],
        out_specs=(pl.BlockSpec(memory_space=pl.ANY), pl.BlockSpec(memory_space=pl.ANY)),
        scratch_shapes=[pltpu.VMEM((KPLANE, ROWS, 512), jnp.bfloat16)] * 7
        + [pltpu.VMEM((ROWS, 128), jnp.bfloat16)] * 7
        + [
            pltpu.VMEM((NZ, NXY, KCHIP, ROWS, 512), jnp.bfloat16),
            dma((NZ,)), dma((NZ,)), dma((NZ, NXY)), dma((NZ, NXY)), dma((NZ,)), dma((NZ,)),
            dma((NZ,)), dma((NZ,)), dma((NZ, NXY)), dma((NZ, NXY)), dma((NZ, 2)), dma((NZ,)), dma((NZ,)),
        ],
        compiler_params=pltpu.CompilerParams(
            collective_id=1, has_side_effects=True, vmem_limit_bytes=48 << 20
        ),
    )(sel, rows, ids)


TILE_I, TILE_J = 256, 512


def maxima_kernel(info_ref, left_ref, right_ref, ids_ref, best_ref, id_col, id_row, col_max):
    e = pl.program_id(0)
    length = 2048

    @pl.when(e == 0)
    def _():
        best_ref[...] = jnp.full((8, length), -1.0, jnp.float32)

    @pl.when(info_ref[e] > 0)
    def _():
        la, lb = info_ref[4 + e], info_ref[8 + e]
        ka, kb = info_ref[12 + e], info_ref[16 + e]
        same = (la == lb).astype(jnp.int32)
        lane = lax.broadcasted_iota(jnp.int32, (length, 128), 1)
        ids = ids_ref[...]
        picked = jnp.where(lane == ka, ids.astype(jnp.float32), 0.0)
        id_col[...] = jnp.sum(picked, axis=1, keepdims=True)
        hot = (lax.broadcasted_iota(jnp.int32, (8, 128), 1) == kb).astype(jnp.bfloat16)
        id_row[...] = lax.dot_general(hot, ids, (((1,), (1,)), ((), ())), preferred_element_type=jnp.float32)
        col_max[...] = jnp.full((8, length), -1.0, jnp.float32)
        for i in range(length // TILE_I):
            half, at = divmod(i * TILE_I, length // 2)
            piece = left_ref[half, 0, at:at + TILE_I, :]
            ida = id_col[i * TILE_I:(i + 1) * TILE_I, :]
            row_max = jnp.full((TILE_I, 128), -1.0, jnp.float32)
            for j in range(length // TILE_J):
                half_j, at_j = divmod(j * TILE_J, length // 2)
                other = right_ref[half_j, 0, at_j:at_j + TILE_J, :]
                gram = lax.dot_general(
                    piece, other, (((1,), (1,)), ((), ())), preferred_element_type=jnp.float32
                )
                keep = ida == id_row[0:1, j * TILE_J:(j + 1) * TILE_J]
                masked = jnp.where(keep, gram, -1.0)
                if i * TILE_I // TILE_J == j:
                    rows = lax.broadcasted_iota(jnp.int32, (TILE_I, TILE_J), 0) + i * TILE_I
                    cols = lax.broadcasted_iota(jnp.int32, (TILE_I, TILE_J), 1) + j * TILE_J
                    masked = jnp.where((rows == cols) & (same == 1), -1.0, masked)
                for g in range(TILE_J // 128):
                    row_max = jnp.maximum(row_max, masked[:, g * 128:(g + 1) * 128])
                span = slice(j * TILE_J, (j + 1) * TILE_J)
                col_max[:, span] = jnp.maximum(
                    col_max[:, span], jnp.max(masked.reshape(TILE_I // 8, 8, TILE_J), axis=0)
                )
            across = jnp.max(jnp.transpose(row_max), axis=0, keepdims=True)
            span = slice(i * TILE_I, (i + 1) * TILE_I)
            best_ref[pl.ds(la, 1), span] = jnp.maximum(best_ref[pl.ds(la, 1), span], across)
        down = jnp.max(col_max[...], axis=0, keepdims=True)
        best_ref[pl.ds(lb, 1), :] = jnp.maximum(best_ref[pl.ds(lb, 1), :], down)


def maxima(info, blocks, ids):
    block = (NC, 1, 1024, 512)
    return pl.pallas_call(
        maxima_kernel,
        grid_spec=pltpu.PrefetchScalarGridSpec(
            num_scalar_prefetch=1,
            grid=(EDGES // NC,),
            in_specs=[
                pl.BlockSpec(block, lambda e, s: (0, s[4 + e], 0, 0)),
                pl.BlockSpec(block, lambda e, s: (0, s[8 + e], 0, 0)),
                pl.BlockSpec((2048, 128), lambda e, s: (0, 0)),
            ],
            out_specs=pl.BlockSpec((8, 2048), lambda e, s: (0, 0)),
            scratch_shapes=[
                pltpu.VMEM((2048, 1), jnp.float32),
                pltpu.VMEM((8, 2048), jnp.float32),
                pltpu.VMEM((8, 2048), jnp.float32),
            ],
        ),
        out_shape=jax.ShapeDtypeStruct((8, 2048), jnp.float32),
        compiler_params=pltpu.CompilerParams(
            dimension_semantics=("arbitrary",), vmem_limit_bytes=40 << 20
        ),
    )(info, blocks, blocks, ids)


def planned(embeddings, cluster_ids, block_slot, plan):
    plane_nodes, local, entry, chips, edge_count = plan
    store, y = lax.axis_index("store"), lax.axis_index("grp")
    x, z, c = store // 16, (store // 2) % 8, store % 2
    slots = jnp.take(block_slot, plane_nodes.reshape(-1))
    rows = pack(embeddings, slots)
    ids = jnp.take(cluster_ids, slots, axis=1).astype(jnp.bfloat16)
    ids = jnp.transpose(ids.reshape(ROWS, NZ, KPLANE), (1, 0, 2))
    ids = jnp.pad(ids, ((0, 0), (0, 0), (0, 128 - KPLANE)))
    sel = lax.dynamic_index_in_dim(local, z, 0, keepdims=False)
    blocks, block_ids = spread(sel, rows, ids)
    blocks = blocks.reshape(NC, KCHIP, 1024, 512)
    block_ids = block_ids.reshape(2048, 128)
    chip = x * 4 + y
    mine = chips[z, chip]
    count = edge_count[z, chip]
    edge = jnp.arange(EDGES // NC) * NC + c
    la, lb = jnp.take(mine, 8 + edge), jnp.take(mine, 16 + edge)
    where = lax.dynamic_slice_in_dim(sel, chip * KCHIP, KCHIP, 0)
    live = edge < count
    la, lb = jnp.where(live, la, 0), jnp.where(live, lb, 0)
    fields = [live.astype(jnp.int32), la, lb, jnp.take(where, la), jnp.take(where, lb)]
    info = jnp.concatenate([jnp.pad(f, (0, 1)) for f in fields]).astype(jnp.int32)
    best = maxima(info, blocks, block_ids)
    best = best[:KCHIP].reshape(KCHIP, NC, NZ, 4, 4, ROWS)
    step = lambda size, at: (at - jnp.arange(size)) % size
    best = jnp.take(best, step(NC, c), axis=1)
    best = jnp.take(best, step(NZ, z), axis=2)
    best = jnp.take(best, step(4, x), axis=3)
    best = jnp.take(best, step(4, y), axis=4)
    best = jnp.transpose(best, (3, 2, 1, 4, 5, 0)).reshape(64, 4, ROWS * KCHIP)
    got = exchange_small(best)
    got = got.reshape(4, 8, 2, 4, ROWS, KCHIP).max(axis=2)
    got = jnp.transpose(got, (3, 1, 0, 2, 4)).reshape(ROWS, NZ * NXY * KCHIP)
    entry_slot = jnp.take(block_slot, jnp.maximum(entry.reshape(-1), 0))
    entry_slot = jnp.where(entry.reshape(-1) >= 0, entry_slot, -1)
    count = block_slot.shape[0]
    match = entry_slot[:, None] == jnp.arange(count)[None, :]
    return jnp.max(jnp.where(match[None], got[:, :, None], jnp.float32(-1.0)), axis=1)


def exchange_small(best):
    best = lax.all_to_all(best, "store", split_axis=0, concat_axis=0, tiled=True)
    return lax.all_to_all(best, "grp", split_axis=1, concat_axis=1, tiled=True)


def body(embeddings, cluster_ids, block_slot, pairs):
    needed = pairs.reshape(-1)
    every_need = lax.all_gather(needed, ("store", "grp"), axis=0, tiled=True)
    both = every_need.reshape(-1, 2)
    sets, few_sets = chip_sets(both[:, 0], both[:, 1])
    *plan, fits = plane_sets(sets)
    return lax.cond(
        few_sets & fits,
        lambda: planned(embeddings, cluster_ids, block_slot, plan),
        lambda: any_pairs(embeddings, cluster_ids, block_slot, every_need, needed),
    )


def solution(mesh):
    return jax.shard_map(
        body,
        mesh=mesh,
        in_specs=(
            P(("store", "grp"), None, None),
            P(("store", "grp"), None),
            P(),
            P(("store", "grp"), None),
        ),
        out_specs=P(("store", "grp"), None),
        check_vma=False,
    )
```

```python
import jax
import jax.numpy as jnp
from jax import lax
from jax.experimental import pallas as pl
from jax.experimental.pallas import tpu as pltpu
from jax.sharding import PartitionSpec as P

MESH = pl.DeviceIdType.MESH
NZ, NXY, NC = 8, 16, 2
KCHIP = 6
EDGES = 6
KPLANE = 64
SETS = NZ * NXY
ROWS = 8


def pair_maxima(left, right, left_ids, right_ids, same):
    length = left.shape[0]
    step_rows = min(512, length)
    columns = jnp.arange(length)

    def row_block(start):
        piece = lax.dynamic_slice_in_dim(left, start, step_rows, 0)
        piece_ids = lax.dynamic_slice_in_dim(left_ids, start, step_rows, 0)
        gram = lax.dot_general(
            piece, right, (((1,), (1,)), ((), ())), preferred_element_type=jnp.float32
        )
        rows = start + jnp.arange(step_rows)
        keep = (piece_ids[:, None] == right_ids[None, :]) & jnp.logical_not(
            same & (rows[:, None] == columns[None, :])
        )
        masked = jnp.where(keep, gram, jnp.float32(-1.0))
        return (jnp.max(masked, axis=1), jnp.max(masked, axis=0))

    starts = jnp.arange(length // step_rows) * step_rows
    row_best, col_best = lax.map(row_block, starts)
    return (row_best.reshape(length), jnp.max(col_best, axis=0))


def any_pairs(embeddings, cluster_ids, block_slot, needed):
    tile_rows, count, width = embeddings.shape
    n_store = lax.axis_size("store")
    n_grp = lax.axis_size("grp")
    length = tile_rows * n_store * n_grp
    norms = lax.rsqrt(jnp.sum(embeddings * embeddings, axis=-1, keepdims=True) + jnp.float32(1e-06))
    unit = jnp.transpose((embeddings * norms).astype(jnp.bfloat16), (1, 0, 2))
    ids_by_slot = cluster_ids.T
    slots_needed = needed.shape[0]
    every_need = lax.all_gather(needed, ("store", "grp"), axis=0, tiled=True)
    asked = jnp.transpose(every_need.reshape(n_store, n_grp, slots_needed), (2, 0, 1))
    asked_slots = jnp.take(block_slot, asked)
    send_rows = jnp.take(unit, asked_slots, axis=0)
    send_ids = jnp.take(ids_by_slot, asked_slots, axis=0)

    def exchange(rows):
        rows = lax.all_to_all(rows, "store", split_axis=1, concat_axis=1, tiled=True)
        return lax.all_to_all(rows, "grp", split_axis=2, concat_axis=2, tiled=True)

    blocks = exchange(send_rows).reshape(slots_needed, length, width)
    block_ids = exchange(send_ids).reshape(slots_needed, length)
    results = []
    for index in range(slots_needed // 2):
        same = needed[2 * index] == needed[2 * index + 1]
        results += pair_maxima(
            blocks[2 * index], blocks[2 * index + 1], block_ids[2 * index], block_ids[2 * index + 1], same
        )
    maxima = jnp.stack(results, axis=0)
    table = jnp.full((count, length), -1.0, jnp.float32).at[needed].max(maxima)
    table = lax.pmax(table, ("store", "grp"))
    position = lax.axis_index(("store", "grp"))
    mine = lax.dynamic_slice_in_dim(table, position * tile_rows, tile_rows, 1)
    return jnp.zeros((tile_rows, count), jnp.float32).at[:, block_slot].set(mine.T)


def position():
    store, y = lax.axis_index("store"), lax.axis_index("grp")
    return store // 16, (store // 2) % 8, store % 2, y


def stepped(dx, dy, dz, dc):
    x, z, c, y = position()
    return ((((x + dx) % 4) * 8 + (z + dz) % 8) * 2 + (c + dc) % 2, (y + dy) % 4)


STEPS_XY = [(dx, dy) for dx in range(4) for dy in range(4)]


def greet():
    peers = [stepped(0, 0, dz, 0) for dz in range(1, NZ)]
    peers += [stepped(dx, dy, 0, 0) for dx, dy in STEPS_XY[1:]]
    peers += [stepped(0, 0, 0, 1)]
    barrier = pltpu.get_barrier_semaphore()
    for peer in peers:
        pl.semaphore_signal(barrier, inc=1, device_id=peer, device_id_type=MESH)
    pl.semaphore_wait(barrier, len(peers))


def send(src, dst, send_sem, recv_sem, step):
    copy = pltpu.make_async_remote_copy(
        src_ref=src, dst_ref=dst, send_sem=send_sem, recv_sem=recv_sem,
        device_id=stepped(*step), device_id_type=MESH,
    )
    copy.start()
    return copy


def gather_kernel(mine_ref, out_ref, zsend, zrecv, psend, precv, csend, crecv):
    greet()
    out_ref[0, 0, 0] = mine_ref[...]
    copies = [
        send(mine_ref, out_ref.at[0, 0, dz], zsend.at[dz], zrecv.at[dz], (0, 0, dz, 0)) for dz in range(1, NZ)
    ]
    for copy in copies:
        copy.wait()
    copies = [
        send(out_ref.at[0, 0], out_ref.at[0, d], psend.at[d], precv.at[d], (dx, dy, 0, 0))
        for d, (dx, dy) in enumerate(STEPS_XY) if d
    ]
    for copy in copies:
        copy.wait()
    send(out_ref.at[0], out_ref.at[1], csend, crecv, (0, 0, 0, 1)).wait()


def gather_pairs(needed):
    dma = pltpu.SemaphoreType.DMA
    mine = jnp.pad(needed, (0, 128 - needed.shape[0])).reshape(1, 128)
    every = pl.pallas_call(
        gather_kernel,
        out_shape=jax.ShapeDtypeStruct((NC, NXY, NZ, 1, 128), jnp.int32),
        in_specs=[pl.BlockSpec(memory_space=pltpu.VMEM)],
        out_specs=pl.BlockSpec(memory_space=pltpu.VMEM),
        scratch_shapes=[dma((NZ,)), dma((NZ,)), dma((NXY,)), dma((NXY,)), dma, dma],
        compiler_params=pltpu.CompilerParams(collective_id=0, has_side_effects=True),
    )(mine)
    return every.reshape(NC * SETS, 128)


def plan_kernel(
    pairs_ref, slot_ref, slots_out, slots_smem, local_smem, info_smem, entry_out, ok_smem,
    table, sets, chips, buf, buf_smem, chip_smem, sem,
):
    n = 512
    f32, i32 = jnp.float32, jnp.int32

    def iota(shape, dim):
        return lax.broadcasted_iota(i32, shape, dim)

    def to_smem(value, ref):
        buf[...] = jnp.zeros((8, n), i32)
        buf[0:value.shape[0], 0:value.shape[1]] = value
        copy = pltpu.make_async_copy(buf, ref, sem)
        copy.start()
        copy.wait()

    got = pairs_ref[...]
    turned = jnp.transpose(got.astype(f32)).astype(i32)
    first_r = jnp.concatenate([turned[0:1], turned[2:3]], axis=1)
    second_r = jnp.concatenate([turned[1:2], turned[3:4]], axis=1)
    first_c = jnp.concatenate([got[:, 0:1], got[:, 2:3]], axis=0)
    second_c = jnp.concatenate([got[:, 1:2], got[:, 3:4]], axis=0)
    key_r, key_c = second_r * n + first_r, second_c * n + first_c
    tie_r, tie_c = key_r * n + iota((1, n), 1), key_c * n + iota((n, 1), 0)
    rank_c = jnp.sum((tie_r < tie_c).astype(f32), axis=1, keepdims=True)
    at = iota((n, n), 1).astype(f32)
    key = jnp.sum(jnp.where(rank_c == at, key_c.astype(f32), 0.0), axis=0, keepdims=True).astype(i32)
    key = jnp.broadcast_to(key, (8, n))
    a, b = key & (n - 1), key >> 9

    lane = iota((8, n), 1)
    sub = iota((8, n), 0)
    nodes = [jnp.full((8, n), -1, i32)] * KCHIP
    count = jnp.zeros((8, n), i32)
    alive = jnp.ones((8, n), i32)
    length = jnp.zeros((8, n), i32)
    left_at = jnp.zeros((8, n), i32)
    right_at = jnp.zeros((8, n), i32)
    for w in range(EDGES):
        aw = a if w == 0 else pltpu.roll(a, n - w, 1)
        bw = b if w == 0 else pltpu.roll(b, n - w, 1)
        at_a = jnp.full((8, n), -1, i32)
        at_b = jnp.full((8, n), -1, i32)
        for m, v in enumerate(nodes):
            at_a = jnp.where(v == aw, m, at_a)
            at_b = jnp.where(v == bw, m, at_b)
        new_a = (at_a < 0).astype(i32)
        new_b = jnp.where((at_b < 0) & (aw != bw), 1, 0)
        la = jnp.where(at_a < 0, count, at_a)
        after = count + new_a
        lb = jnp.where(aw == bw, la, jnp.where(at_b < 0, after, at_b))
        total = after + new_b
        alive = jnp.where((total <= KCHIP) & (lane + w < n), alive, 0)
        put_a, put_b = alive * new_a, alive * new_b
        nodes = [
            jnp.where((put_a == 1) & (la == m), aw, jnp.where((put_b == 1) & (lb == m), bw, v))
            for m, v in enumerate(nodes)
        ]
        count = jnp.where(alive == 1, total, count)
        length = length + alive
        left_at = jnp.where(sub == w, la, left_at)
        right_at = jnp.where(sub == w, lb, right_at)
    held = jnp.full((8, n), -1, i32)
    for m, v in enumerate(nodes):
        held = jnp.where(sub == m, v, held)
    stack = jnp.concatenate([held, left_at, right_at, length], axis=0).astype(f32)
    stack = jnp.concatenate([stack, jnp.zeros((96, n), f32)], axis=0)
    table[0:n, :] = jnp.transpose(stack)
    blank = jnp.where(iota((16, 128), 1) < 8, -1.0, 0.0).astype(f32)
    table[n:n + 8, :] = blank[0:8]
    to_smem(lane + length, buf_smem)

    def one_set(t, carry):
        s, real = carry
        sets[pl.ds(t, 1), :] = table[pl.ds(s, 1), :]
        after = jnp.where(s < n, buf_smem[0, jnp.minimum(s, n - 1)], n)
        return after, real + (s < n).astype(i32)

    last, real = lax.fori_loop(0, SETS, one_set, (i32(0), i32(0)))
    sets[SETS:SETS + 16, :] = blank

    rows = iota((SETS, SETS), 0)
    cols = iota((SETS, SETS), 1)
    by_set = sets[0:SETS, :]
    by_set_t = jnp.transpose(by_set)
    fresh = jnp.zeros((SETS, SETS), f32)
    for m in range(KCHIP):
        col = by_set[:, m:m + 1]
        prev = jnp.full((SETS, SETS), -1, i32)
        for k in range(KCHIP):
            prev = jnp.where((by_set_t[k:k + 1, :] == col) & (cols < rows), jnp.maximum(prev, cols), prev)
        prev = jnp.max(prev.astype(f32), axis=1, keepdims=True)
        fresh = fresh + jnp.where((prev < cols.astype(f32)) & (col >= 0) & (rows >= cols), 1.0, 0.0)
    upto = (cols <= rows).astype(f32).astype(jnp.bfloat16)
    distinct = jnp.dot(upto, fresh.astype(jnp.bfloat16), preferred_element_type=f32)
    fits = jnp.where((rows >= cols) & (rows < cols + NXY) & (distinct <= KPLANE), 1.0, 0.0)
    after = jnp.sum(fits, axis=0, keepdims=True).astype(i32) + iota((1, SETS), 1)
    to_smem(after, buf_smem)
    starts = [0, buf_smem[0, 0]]
    for _ in range(NZ - 1):
        s = starts[-1]
        starts.append(jnp.where(s < SETS, buf_smem[0, jnp.minimum(s, SETS - 1)], SETS))
    ok_smem[0] = jnp.where((last == n) & (starts[NZ] >= real), 1, 0)
    for p in range(NZ):
        part = sets[pl.ds(starts[p], NXY), :]
        chips[p * NXY:(p + 1) * NXY, :] = jnp.where(
            iota((NXY, 128), 0) + starts[p] < starts[p + 1], part, blank
        )

    by_chip = chips[...]
    by_chip_t = jnp.transpose(by_chip)
    plane = (rows >> 4) == (cols >> 4)
    earlier = plane & (rows < cols)
    is_first, ranks = [], []
    total = jnp.zeros((1, SETS), f32)
    for m in range(KCHIP):
        row = by_chip_t[m:m + 1, :]
        seen = jnp.zeros((SETS, SETS), f32)
        for k in range(KCHIP):
            seen = jnp.where((by_chip[:, k:k + 1] == row) & earlier, 1.0, seen)
        seen = jnp.max(seen, axis=0, keepdims=True)
        first = jnp.where((row >= 0) & (seen == 0), 1.0, 0.0)
        is_first.append(first)
        ranks.append(total)
        total = total + first
    before = jnp.dot(
        jnp.broadcast_to(total, (8, SETS)).astype(jnp.bfloat16),
        jnp.where(earlier, 1.0, 0.0).astype(jnp.bfloat16), preferred_element_type=f32,
    )[0:1]
    marks = [jnp.where(f > 0, r + before + 1.0, 0.0) for f, r in zip(is_first, ranks)]
    slot_col = jnp.transpose(jnp.broadcast_to(slot_ref[...].astype(f32), (128, n)))
    block = iota((n, SETS), 0).astype(f32)
    slots = []
    for m in range(KCHIP):
        row = by_chip_t[m:m + 1, :]
        slot = jnp.sum(jnp.where(block == row, slot_col, 0.0), axis=0, keepdims=True)
        slots.append(jnp.where(row >= 0, slot, -1.0))
    pad = [jnp.full((8 - KCHIP, SETS), -1.0, f32)]
    tail = [jnp.zeros((SETS - 16, SETS), f32)]
    both = jnp.transpose(jnp.concatenate(marks + pad + slots + pad + tail, axis=0))
    entry_out[...] = both
    local = []
    for m in range(KCHIP):
        row = by_chip_t[m:m + 1, :]
        where = jnp.zeros((SETS, SETS), f32)
        for k in range(KCHIP):
            where = jnp.where((by_chip[:, k:k + 1] == row) & plane, jnp.maximum(where, both[:, k:k + 1]), where)
        local.append(jnp.maximum(jnp.max(where, axis=0, keepdims=True) - 1.0, 0.0))
    local = jnp.concatenate(local + [jnp.zeros((8 - KCHIP, SETS), f32)], axis=0).astype(i32)
    placed = jnp.zeros((SETS, SETS), f32)
    for m in range(KCHIP):
        placed = placed + jnp.where(both[:, m:m + 1] == cols.astype(f32) + 1.0, both[:, 8 + m:9 + m], 0.0)
    placed = jnp.concatenate(
        [jnp.sum(placed[p * NXY:(p + 1) * NXY], axis=0, keepdims=True) for p in range(NZ)], axis=0
    ).astype(i32)
    slots_out[...] = placed
    to_smem(placed, slots_smem)
    to_smem(local, local_smem)

    x, z, c, y = position()
    chip = z * NXY + x * 4 + y
    mine = chips[pl.ds(chip, 1), :].astype(i32)
    to_smem(mine, chip_smem)
    for e in range(EDGES // NC):
        at = NC * e + c
        live = at < chip_smem[0, 24]
        la = jnp.where(live, chip_smem[0, 8 + at], 0)
        lb = jnp.where(live, chip_smem[0, 16 + at], 0)
        info_smem[e] = live.astype(i32)
        info_smem[4 + e] = la
        info_smem[8 + e] = lb
        info_smem[12 + e] = local_smem[la, chip]
        info_smem[16 + e] = local_smem[lb, chip]


def make_plan(every, block_slot):
    vmem, smem = pl.BlockSpec(memory_space=pltpu.VMEM), pl.BlockSpec(memory_space=pltpu.SMEM)
    i32 = jnp.int32
    shape = jax.ShapeDtypeStruct
    return pl.pallas_call(
        plan_kernel,
        out_shape=(
            shape((NZ, 128), i32), shape((8, 512), i32), shape((8, 512), i32), shape((20,), i32),
            shape((SETS, 128), jnp.float32), shape((1,), i32),
        ),
        in_specs=[vmem, vmem],
        out_specs=(vmem, smem, smem, smem, vmem, smem),
        scratch_shapes=[
            pltpu.VMEM((520, 128), jnp.float32), pltpu.VMEM((SETS + 16, 128), jnp.float32),
            pltpu.VMEM((SETS, 128), jnp.float32), pltpu.VMEM((8, 512), i32), pltpu.SMEM((8, 512), i32),
            pltpu.SMEM((8, 512), i32), pltpu.SemaphoreType.DMA,
        ],
        compiler_params=pltpu.CompilerParams(vmem_limit_bytes=32 << 20),
    )(every, block_slot.reshape(1, -1))


def pack_kernel(slot_ref, slots_ref, cluster_ref, emb_ref, out_ref, ids_ref, raw, sems):
    plane = pl.program_id(0)
    planes = pl.num_programs(0)

    def fetch(p, buf):
        def one(n, carry):
            pltpu.make_async_copy(
                emb_ref.at[:, slot_ref[p, n], :], raw.at[buf, n], sems.at[buf]
            ).start()
            return carry

        lax.fori_loop(0, KPLANE, one, 0, unroll=8)

    @pl.when(plane == 0)
    def _():
        fetch(0, 0)

    buf = lax.rem(plane, 2)

    @pl.when(plane + 1 < planes)
    def _():
        fetch(plane + 1, 1 - buf)

    hot = lax.broadcasted_iota(jnp.int32, (512, 128), 0) == slots_ref[pl.ds(plane, 1), :]
    ids = jnp.dot(
        cluster_ref[...].astype(jnp.bfloat16), jnp.where(hot, 1.0, 0.0).astype(jnp.bfloat16),
        preferred_element_type=jnp.float32,
    )
    ids_ref[0] = ids.astype(jnp.bfloat16)
    pltpu.make_async_copy(raw.at[buf], raw.at[buf], sems.at[buf]).wait()

    def norm(n, carry):
        rows = raw[buf, pl.ds(n * 8, 8)]
        scale = lax.rsqrt(jnp.sum(rows * rows, axis=-1, keepdims=True) + jnp.float32(1e-06))
        out_ref[0, pl.ds(n * 8, 8)] = (rows * scale).astype(jnp.bfloat16)
        return carry

    lax.fori_loop(0, KPLANE // 8, norm, 0)


def pack(embeddings, cluster_ids, slots, slots_smem):
    return pl.pallas_call(
        pack_kernel,
        grid=(NZ,),
        in_specs=[
            pl.BlockSpec(memory_space=pltpu.SMEM),
            pl.BlockSpec((NZ, 128), lambda p: (0, 0)),
            pl.BlockSpec((ROWS, 512), lambda p: (0, 0)),
            pl.BlockSpec(memory_space=pl.ANY),
        ],
        out_specs=(
            pl.BlockSpec((1, KPLANE, ROWS, 512), lambda p: (p, 0, 0, 0)),
            pl.BlockSpec((1, ROWS, 128), lambda p: (p, 0, 0)),
        ),
        scratch_shapes=[
            pltpu.VMEM((2, KPLANE, ROWS, 512), jnp.float32),
            pltpu.SemaphoreType.DMA((2,)),
        ],
        out_shape=(
            jax.ShapeDtypeStruct((NZ, KPLANE, ROWS, 512), jnp.bfloat16),
            jax.ShapeDtypeStruct((NZ, ROWS, 128), jnp.bfloat16),
        ),
        compiler_params=pltpu.CompilerParams(
            dimension_semantics=("arbitrary",), vmem_limit_bytes=32 << 20
        ),
    )(slots_smem, slots, cluster_ids, embeddings)


Z_ORDER = (1, 7, 2, 6, 3, 5, 4)


def spread_kernel(sel_ref, rows_ref, ids_ref, out_ref, idout_ref, *scratch):
    land = scratch[:7]
    idland = scratch[7:14]
    pick, zsend, zrecv, psend, precv, csend, crecv, isend, irecv, jsend, jrecv, local_sem, bsend, brecv = scratch[14:]
    x, z, c, y = position()
    device = stepped
    greet()

    z_copies = {}
    for dz in Z_ORDER:
        rows = pltpu.make_async_remote_copy(
            src_ref=rows_ref.at[(z + dz) % 8], dst_ref=land[dz - 1],
            send_sem=zsend.at[dz], recv_sem=zrecv.at[dz],
            device_id=device(0, 0, dz, 0), device_id_type=MESH,
        )
        ids = pltpu.make_async_remote_copy(
            src_ref=ids_ref.at[(z + dz) % 8], dst_ref=idland[dz - 1],
            send_sem=isend.at[dz], recv_sem=irecv.at[dz],
            device_id=device(0, 0, dz, 0), device_id_type=MESH,
        )
        ids.start()
        rows.start()
        z_copies[dz] = (rows, ids)

    p_copies = {}
    c_copies = {}
    l_copies = {}

    def plane_send(dz):
        if dz == 0:
            def chip(q, carry):
                for n in range(KCHIP):
                    pick[0, q, n] = rows_ref[z, sel_ref[n, z * NXY + q]]
                return carry
            id_src = ids_ref.at[z]
        else:
            rows, ids = z_copies[dz]
            rows.wait_recv()
            ids.wait_recv()

            def chip(q, carry):
                for n in range(KCHIP):
                    pick[dz, q, n] = land[dz - 1][sel_ref[n, z * NXY + q]]
                return carry
            id_src = idland[dz - 1]
        lax.fori_loop(0, NXY, chip, 0)
        copies = []
        for dx in range(4):
            for dy in range(4):
                d = dx * 4 + dy
                q = ((x + dx) % 4) * 4 + (y + dy) % 4
                if d == 0:
                    one = pltpu.make_async_copy(pick.at[dz, q], out_ref.at[0, :, 0, dz], local_sem.at[dz, 0])
                    two = pltpu.make_async_copy(id_src, idout_ref.at[0, 0, dz], local_sem.at[dz, 1])
                    one.start()
                    two.start()
                    l_copies[dz] = (one, two)
                    continue
                one = pltpu.make_async_remote_copy(
                    src_ref=pick.at[dz, q], dst_ref=out_ref.at[0, :, d, dz],
                    send_sem=psend.at[dz, d], recv_sem=precv.at[dz, d],
                    device_id=device(dx, dy, 0, 0), device_id_type=MESH,
                )
                two = pltpu.make_async_remote_copy(
                    src_ref=id_src, dst_ref=idout_ref.at[0, d, dz],
                    send_sem=jsend.at[dz, d], recv_sem=jrecv.at[dz, d],
                    device_id=device(dx, dy, 0, 0), device_id_type=MESH,
                )
                two.start()
                one.start()
                copies += [one, two]
        p_copies[dz] = copies

    def core_send(dz):
        for copy in p_copies[dz]:
            copy.wait_recv()
        for copy in l_copies[dz]:
            copy.wait()
        one = pltpu.make_async_remote_copy(
            src_ref=out_ref.at[0, :, :, dz], dst_ref=out_ref.at[1, :, :, dz],
            send_sem=csend.at[dz], recv_sem=crecv.at[dz],
            device_id=device(0, 0, 0, 1), device_id_type=MESH,
        )
        two = pltpu.make_async_remote_copy(
            src_ref=idout_ref.at[0, :, dz], dst_ref=idout_ref.at[1, :, dz],
            send_sem=bsend.at[dz], recv_sem=brecv.at[dz],
            device_id=device(0, 0, 0, 1), device_id_type=MESH,
        )
        one.start()
        two.start()
        c_copies[dz] = (one, two)

    order = (0,) + Z_ORDER
    for i, dz in enumerate(order):
        plane_send(dz)
        if i >= 2:
            core_send(order[i - 2])
    core_send(order[-2])
    core_send(order[-1])
    for dz in order:
        for copy in c_copies[dz]:
            copy.wait()
        for copy in p_copies[dz]:
            copy.wait_send()
        if dz:
            for copy in z_copies[dz]:
                copy.wait_send()


def spread(sel, rows, ids):
    dma = pltpu.SemaphoreType.DMA
    return pl.pallas_call(
        spread_kernel,
        out_shape=(
            jax.ShapeDtypeStruct((NC, KCHIP, NXY, NZ, ROWS, 512), jnp.bfloat16),
            jax.ShapeDtypeStruct((NC, NXY, NZ, ROWS, 128), jnp.bfloat16),
        ),
        in_specs=[
            pl.BlockSpec(memory_space=pltpu.SMEM),
            pl.BlockSpec(memory_space=pltpu.VMEM),
            pl.BlockSpec(memory_space=pltpu.VMEM),
        ],
        out_specs=(pl.BlockSpec(memory_space=pl.ANY), pl.BlockSpec(memory_space=pl.ANY)),
        scratch_shapes=[pltpu.VMEM((KPLANE, ROWS, 512), jnp.bfloat16)] * 7
        + [pltpu.VMEM((ROWS, 128), jnp.bfloat16)] * 7
        + [
            pltpu.VMEM((NZ, NXY, KCHIP, ROWS, 512), jnp.bfloat16),
            dma((NZ,)), dma((NZ,)), dma((NZ, NXY)), dma((NZ, NXY)), dma((NZ,)), dma((NZ,)),
            dma((NZ,)), dma((NZ,)), dma((NZ, NXY)), dma((NZ, NXY)), dma((NZ, 2)), dma((NZ,)), dma((NZ,)),
        ],
        compiler_params=pltpu.CompilerParams(
            collective_id=1, has_side_effects=True, vmem_limit_bytes=48 << 20
        ),
    )(sel, rows, ids)


TILE_I, TILE_J = 256, 512


def maxima_kernel(info_ref, left_ref, right_ref, ids_ref, best_ref, id_col, id_row, col_max):
    e = pl.program_id(0)
    length = 2048

    @pl.when(e == 0)
    def _():
        best_ref[...] = jnp.full((8, length), -1.0, jnp.float32)

    @pl.when(info_ref[e] > 0)
    def _():
        la, lb = info_ref[4 + e], info_ref[8 + e]
        ka, kb = info_ref[12 + e], info_ref[16 + e]
        same = (la == lb).astype(jnp.int32)
        lane = lax.broadcasted_iota(jnp.int32, (length, 128), 1)
        ids = ids_ref[...]
        picked = jnp.where(lane == ka, ids.astype(jnp.float32), 0.0)
        id_col[...] = jnp.sum(picked, axis=1, keepdims=True)
        hot = (lax.broadcasted_iota(jnp.int32, (8, 128), 1) == kb).astype(jnp.bfloat16)
        id_row[...] = lax.dot_general(hot, ids, (((1,), (1,)), ((), ())), preferred_element_type=jnp.float32)
        col_max[...] = jnp.full((8, length), -1.0, jnp.float32)
        for i in range(length // TILE_I):
            half, at = divmod(i * TILE_I, length // 2)
            piece = left_ref[half, 0, at:at + TILE_I, :]
            ida = id_col[i * TILE_I:(i + 1) * TILE_I, :]
            row_max = jnp.full((TILE_I, 128), -1.0, jnp.float32)
            for j in range(length // TILE_J):
                half_j, at_j = divmod(j * TILE_J, length // 2)
                other = right_ref[half_j, 0, at_j:at_j + TILE_J, :]
                gram = lax.dot_general(
                    piece, other, (((1,), (1,)), ((), ())), preferred_element_type=jnp.float32
                )
                keep = ida == id_row[0:1, j * TILE_J:(j + 1) * TILE_J]
                masked = jnp.where(keep, gram, -1.0)
                if i * TILE_I // TILE_J == j:
                    rows = lax.broadcasted_iota(jnp.int32, (TILE_I, TILE_J), 0) + i * TILE_I
                    cols = lax.broadcasted_iota(jnp.int32, (TILE_I, TILE_J), 1) + j * TILE_J
                    masked = jnp.where((rows == cols) & (same == 1), -1.0, masked)
                for g in range(TILE_J // 128):
                    row_max = jnp.maximum(row_max, masked[:, g * 128:(g + 1) * 128])
                span = slice(j * TILE_J, (j + 1) * TILE_J)
                col_max[:, span] = jnp.maximum(
                    col_max[:, span], jnp.max(masked.reshape(TILE_I // 8, 8, TILE_J), axis=0)
                )
            across = jnp.max(jnp.transpose(row_max), axis=0, keepdims=True)
            span = slice(i * TILE_I, (i + 1) * TILE_I)
            best_ref[pl.ds(la, 1), span] = jnp.maximum(best_ref[pl.ds(la, 1), span], across)
        down = jnp.max(col_max[...], axis=0, keepdims=True)
        best_ref[pl.ds(lb, 1), :] = jnp.maximum(best_ref[pl.ds(lb, 1), :], down)


def maxima(info, blocks, ids):
    block = (NC, 1, 1024, 512)
    return pl.pallas_call(
        maxima_kernel,
        grid_spec=pltpu.PrefetchScalarGridSpec(
            num_scalar_prefetch=1,
            grid=(EDGES // NC,),
            in_specs=[
                pl.BlockSpec(block, lambda e, s: (0, s[4 + e], 0, 0)),
                pl.BlockSpec(block, lambda e, s: (0, s[8 + e], 0, 0)),
                pl.BlockSpec((2048, 128), lambda e, s: (0, 0)),
            ],
            out_specs=pl.BlockSpec((8, 2048), lambda e, s: (0, 0)),
            scratch_shapes=[
                pltpu.VMEM((2048, 1), jnp.float32),
                pltpu.VMEM((8, 2048), jnp.float32),
                pltpu.VMEM((8, 2048), jnp.float32),
            ],
        ),
        out_shape=jax.ShapeDtypeStruct((8, 2048), jnp.float32),
        compiler_params=pltpu.CompilerParams(
            dimension_semantics=("arbitrary",), vmem_limit_bytes=40 << 20
        ),
    )(info, blocks, blocks, ids)


def return_kernel(best_ref, out_ref, other, merged, stage, land, table, turned, tiles, csend, crecv, psend, precv, zsend, zrecv):
    x, z, c, y = position()
    greet()
    half = SETS * ROWS
    send(best_ref.at[:, half:], other, csend, crecv, (0, 0, 0, 1)).wait()
    merged[...] = jnp.maximum(best_ref[:, :half], other[...])
    stage[...] = jnp.zeros((NXY, 8, 128), jnp.float32)
    for d in range(NXY):
        stage[d, :, 0:64] = merged[:, d * 64:(d + 1) * 64]
    copies = [
        send(stage.at[d], land.at[d], psend.at[d], precv.at[d], (-dx, -dy, 0, 0))
        for d, (dx, dy) in enumerate(STEPS_XY) if d
    ]
    table[:, x * 4 + y, :] = stage[0]
    for copy in copies:
        copy.wait()
    for d, (dx, dy) in enumerate(STEPS_XY):
        if d:
            table[:, ((x + dx) % 4) * 4 + (y + dy) % 4, :] = land[d]
    turned[...] = jnp.transpose(table[...].reshape(8 * NXY, 128))
    copies = [
        send(turned.at[pl.ds(dz * 8, 8)], tiles.at[dz], zsend.at[dz], zrecv.at[dz], (0, 0, -dz, 0))
        for dz in range(1, NZ)
    ]
    out_ref[z] = turned[0:8, :]
    for copy in copies:
        copy.wait()
    for dz in range(1, NZ):
        out_ref[(z + dz) % 8] = tiles[dz]


def give_back(best):
    dma = pltpu.SemaphoreType.DMA
    f32 = jnp.float32
    return pl.pallas_call(
        return_kernel,
        out_shape=jax.ShapeDtypeStruct((NZ, ROWS, 128), f32),
        in_specs=[pl.BlockSpec(memory_space=pltpu.VMEM)],
        out_specs=pl.BlockSpec(memory_space=pltpu.VMEM),
        scratch_shapes=[
            pltpu.VMEM((8, SETS * ROWS), f32), pltpu.VMEM((8, SETS * ROWS), f32), pltpu.VMEM((NXY, 8, 128), f32),
            pltpu.VMEM((NXY, 8, 128), f32), pltpu.VMEM((8, NXY, 128), f32), pltpu.VMEM((128, 128), f32),
            pltpu.VMEM((NZ, ROWS, 128), f32),
            dma, dma, dma((NXY,)), dma((NXY,)), dma((NZ,)), dma((NZ,)),
        ],
        compiler_params=pltpu.CompilerParams(collective_id=2, has_side_effects=True, vmem_limit_bytes=16 << 20),
    )(best)


def combine_kernel(got_ref, entry_ref, out_ref):
    count = out_ref.shape[1]
    out = [jnp.full((8, count), -1.0, jnp.float32) for _ in range(ROWS)]
    column = lax.broadcasted_iota(jnp.int32, (128, count), 1).astype(jnp.float32)
    for z in range(NZ):
        values = jnp.transpose(jnp.concatenate([got_ref[z], jnp.zeros((120, 128), jnp.float32)], axis=0))
        slot = jnp.concatenate(
            [entry_ref[z * NXY:(z + 1) * NXY, 8 + n:9 + n] for n in range(8)], axis=0
        )
        match = slot == column
        for r in range(ROWS):
            best = jnp.where(match, values[:, r:r + 1], -1.0)
            out[r] = jnp.maximum(out[r], jnp.max(best.reshape(16, 8, count), axis=0))
    out_ref[...] = jnp.concatenate([jnp.max(o, axis=0, keepdims=True) for o in out], axis=0)


def combine(got, entry, count):
    return pl.pallas_call(
        combine_kernel,
        out_shape=jax.ShapeDtypeStruct((ROWS, count), jnp.float32),
        in_specs=[pl.BlockSpec(memory_space=pltpu.VMEM)] * 2,
        out_specs=pl.BlockSpec(memory_space=pltpu.VMEM),
        compiler_params=pltpu.CompilerParams(vmem_limit_bytes=16 << 20),
    )(got, entry)


def planned(embeddings, cluster_ids, block_slot, plan):
    slots, slots_smem, local, info, entry = plan
    rows, ids = pack(embeddings, cluster_ids, slots, slots_smem)
    blocks, block_ids = spread(local, rows, ids)
    best = maxima(info, blocks.reshape(NC, KCHIP, 1024, 512), block_ids.reshape(2048, 128))
    return combine(give_back(best), entry, block_slot.shape[0])


def body(embeddings, cluster_ids, block_slot, pairs):
    needed = pairs.reshape(-1)
    *plan, ok = make_plan(gather_pairs(needed), block_slot)
    return lax.cond(
        ok[0] == 1,
        lambda: planned(embeddings, cluster_ids, block_slot, plan),
        lambda: any_pairs(embeddings, cluster_ids, block_slot, needed),
    )


def solution(mesh):
    return jax.shard_map(
        body,
        mesh=mesh,
        in_specs=(
            P(("store", "grp"), None, None),
            P(("store", "grp"), None),
            P(),
            P(("store", "grp"), None),
        ),
        out_specs=P(("store", "grp"), None),
        check_vma=False,
    )
```

```python
import jax
import jax.numpy as jnp
from jax import lax
from jax.experimental import pallas as pl
from jax.experimental.pallas import tpu as pltpu
from jax.sharding import PartitionSpec as P

MESH = pl.DeviceIdType.MESH
NZ, NXY, NC = 8, 16, 2
KCHIP = 6
EDGES = 6
KPLANES = (56, 60, 64)
SETS = NZ * NXY
ROWS = 8


def pair_maxima(left, right, left_ids, right_ids, same):
    length = left.shape[0]
    step_rows = min(512, length)
    columns = jnp.arange(length)

    def row_block(start):
        piece = lax.dynamic_slice_in_dim(left, start, step_rows, 0)
        piece_ids = lax.dynamic_slice_in_dim(left_ids, start, step_rows, 0)
        gram = lax.dot_general(
            piece, right, (((1,), (1,)), ((), ())), preferred_element_type=jnp.float32
        )
        rows = start + jnp.arange(step_rows)
        keep = (piece_ids[:, None] == right_ids[None, :]) & jnp.logical_not(
            same & (rows[:, None] == columns[None, :])
        )
        masked = jnp.where(keep, gram, jnp.float32(-1.0))
        return (jnp.max(masked, axis=1), jnp.max(masked, axis=0))

    starts = jnp.arange(length // step_rows) * step_rows
    row_best, col_best = lax.map(row_block, starts)
    return (row_best.reshape(length), jnp.max(col_best, axis=0))


def any_pairs(embeddings, cluster_ids, block_slot, needed):
    tile_rows, count, width = embeddings.shape
    n_store = lax.axis_size("store")
    n_grp = lax.axis_size("grp")
    length = tile_rows * n_store * n_grp
    norms = lax.rsqrt(jnp.sum(embeddings * embeddings, axis=-1, keepdims=True) + jnp.float32(1e-06))
    unit = jnp.transpose((embeddings * norms).astype(jnp.bfloat16), (1, 0, 2))
    ids_by_slot = cluster_ids.T
    slots_needed = needed.shape[0]
    every_need = lax.all_gather(needed, ("store", "grp"), axis=0, tiled=True)
    asked = jnp.transpose(every_need.reshape(n_store, n_grp, slots_needed), (2, 0, 1))
    asked_slots = jnp.take(block_slot, asked)
    send_rows = jnp.take(unit, asked_slots, axis=0)
    send_ids = jnp.take(ids_by_slot, asked_slots, axis=0)

    def exchange(rows):
        rows = lax.all_to_all(rows, "store", split_axis=1, concat_axis=1, tiled=True)
        return lax.all_to_all(rows, "grp", split_axis=2, concat_axis=2, tiled=True)

    blocks = exchange(send_rows).reshape(slots_needed, length, width)
    block_ids = exchange(send_ids).reshape(slots_needed, length)
    results = []
    for index in range(slots_needed // 2):
        same = needed[2 * index] == needed[2 * index + 1]
        results += pair_maxima(
            blocks[2 * index], blocks[2 * index + 1], block_ids[2 * index], block_ids[2 * index + 1], same
        )
    maxima = jnp.stack(results, axis=0)
    table = jnp.full((count, length), -1.0, jnp.float32).at[needed].max(maxima)
    table = lax.pmax(table, ("store", "grp"))
    position = lax.axis_index(("store", "grp"))
    mine = lax.dynamic_slice_in_dim(table, position * tile_rows, tile_rows, 1)
    return jnp.zeros((tile_rows, count), jnp.float32).at[:, block_slot].set(mine.T)


def position():
    store, y = lax.axis_index("store"), lax.axis_index("grp")
    return store // 16, (store // 2) % 8, store % 2, y


def stepped(dx, dy, dz, dc):
    x, z, c, y = position()
    return ((((x + dx) % 4) * 8 + (z + dz) % 8) * 2 + (c + dc) % 2, (y + dy) % 4)


STEPS_XY = [(dx, dy) for dx in range(4) for dy in range(4)]


def greet():
    peers = [stepped(0, 0, dz, 0) for dz in range(1, NZ)]
    peers += [stepped(dx, dy, 0, 0) for dx, dy in STEPS_XY[1:]]
    peers += [stepped(0, 0, 0, 1)]
    barrier = pltpu.get_barrier_semaphore()
    for peer in peers:
        pl.semaphore_signal(barrier, inc=1, device_id=peer, device_id_type=MESH)
    pl.semaphore_wait(barrier, len(peers))


def send(src, dst, send_sem, recv_sem, step):
    copy = pltpu.make_async_remote_copy(
        src_ref=src, dst_ref=dst, send_sem=send_sem, recv_sem=recv_sem,
        device_id=stepped(*step), device_id_type=MESH,
    )
    copy.start()
    return copy


def gather_kernel(mine_ref, out_ref, zsend, zrecv, psend, precv, csend, crecv):
    greet()
    out_ref[0, 0, 0] = mine_ref[...]
    copies = [
        send(mine_ref, out_ref.at[0, 0, dz], zsend.at[dz], zrecv.at[dz], (0, 0, dz, 0)) for dz in range(1, NZ)
    ]
    for copy in copies:
        copy.wait()
    copies = [
        send(out_ref.at[0, 0], out_ref.at[0, d], psend.at[d], precv.at[d], (dx, dy, 0, 0))
        for d, (dx, dy) in enumerate(STEPS_XY) if d
    ]
    for copy in copies:
        copy.wait()
    send(out_ref.at[0], out_ref.at[1], csend, crecv, (0, 0, 0, 1)).wait()


def gather_pairs(needed):
    dma = pltpu.SemaphoreType.DMA
    mine = jnp.pad(needed, (0, 128 - needed.shape[0])).reshape(1, 128)
    every = pl.pallas_call(
        gather_kernel,
        out_shape=jax.ShapeDtypeStruct((NC, NXY, NZ, 1, 128), jnp.int32),
        in_specs=[pl.BlockSpec(memory_space=pltpu.VMEM)],
        out_specs=pl.BlockSpec(memory_space=pltpu.VMEM),
        scratch_shapes=[dma((NZ,)), dma((NZ,)), dma((NXY,)), dma((NXY,)), dma, dma],
        compiler_params=pltpu.CompilerParams(collective_id=0, has_side_effects=True),
    )(mine)
    return every.reshape(NC * SETS, 128)


def plan_kernel(
    pairs_ref, slot_ref, slots_out, slots_smem, local_smem, info_smem, entry_out, ok_smem,
    table, sets, chips, buf, buf_smem, chip_smem, sem,
):
    n = 512
    f32, i32 = jnp.float32, jnp.int32

    def iota(shape, dim):
        return lax.broadcasted_iota(i32, shape, dim)

    def to_smem(value, ref):
        buf[...] = jnp.zeros((8, n), i32)
        buf[0:value.shape[0], 0:value.shape[1]] = value
        copy = pltpu.make_async_copy(buf, ref, sem)
        copy.start()
        copy.wait()

    got = pairs_ref[...]
    turned = jnp.transpose(got.astype(f32)).astype(i32)
    first_r = jnp.concatenate([turned[0:1], turned[2:3]], axis=1)
    second_r = jnp.concatenate([turned[1:2], turned[3:4]], axis=1)
    first_c = jnp.concatenate([got[:, 0:1], got[:, 2:3]], axis=0)
    second_c = jnp.concatenate([got[:, 1:2], got[:, 3:4]], axis=0)
    key_r, key_c = second_r * n + first_r, second_c * n + first_c
    tie_r, tie_c = key_r * n + iota((1, n), 1), key_c * n + iota((n, 1), 0)
    rank_c = jnp.sum((tie_r < tie_c).astype(f32), axis=1, keepdims=True)
    at = iota((n, n), 1).astype(f32)
    key = jnp.sum(jnp.where(rank_c == at, key_c.astype(f32), 0.0), axis=0, keepdims=True).astype(i32)
    key = jnp.broadcast_to(key, (8, n))
    a, b = key & (n - 1), key >> 9

    lane = iota((8, n), 1)
    sub = iota((8, n), 0)
    nodes = [jnp.full((8, n), -1, i32)] * KCHIP
    count = jnp.zeros((8, n), i32)
    alive = jnp.ones((8, n), i32)
    length = jnp.zeros((8, n), i32)
    left_at = jnp.zeros((8, n), i32)
    right_at = jnp.zeros((8, n), i32)
    for w in range(EDGES):
        aw = a if w == 0 else pltpu.roll(a, n - w, 1)
        bw = b if w == 0 else pltpu.roll(b, n - w, 1)
        at_a = jnp.full((8, n), -1, i32)
        at_b = jnp.full((8, n), -1, i32)
        for m, v in enumerate(nodes):
            at_a = jnp.where(v == aw, m, at_a)
            at_b = jnp.where(v == bw, m, at_b)
        new_a = (at_a < 0).astype(i32)
        new_b = jnp.where((at_b < 0) & (aw != bw), 1, 0)
        la = jnp.where(at_a < 0, count, at_a)
        after = count + new_a
        lb = jnp.where(aw == bw, la, jnp.where(at_b < 0, after, at_b))
        total = after + new_b
        alive = jnp.where((total <= KCHIP) & (lane + w < n), alive, 0)
        put_a, put_b = alive * new_a, alive * new_b
        nodes = [
            jnp.where((put_a == 1) & (la == m), aw, jnp.where((put_b == 1) & (lb == m), bw, v))
            for m, v in enumerate(nodes)
        ]
        count = jnp.where(alive == 1, total, count)
        length = length + alive
        left_at = jnp.where(sub == w, la, left_at)
        right_at = jnp.where(sub == w, lb, right_at)
    held = jnp.full((8, n), -1, i32)
    for m, v in enumerate(nodes):
        held = jnp.where(sub == m, v, held)
    stack = jnp.concatenate([held, left_at, right_at, length], axis=0).astype(f32)
    stack = jnp.concatenate([stack, jnp.zeros((96, n), f32)], axis=0)
    table[0:n, :] = jnp.transpose(stack)
    blank = jnp.where(iota((16, 128), 1) < 8, -1.0, 0.0).astype(f32)
    table[n:n + 8, :] = blank[0:8]
    to_smem(lane + length, buf_smem)

    def one_set(t, carry):
        s, real = carry
        sets[pl.ds(t, 1), :] = table[pl.ds(s, 1), :]
        after = jnp.where(s < n, buf_smem[0, jnp.minimum(s, n - 1)], n)
        return after, real + (s < n).astype(i32)

    last, real = lax.fori_loop(0, SETS, one_set, (i32(0), i32(0)))
    sets[SETS:SETS + 16, :] = blank

    rows = iota((SETS, SETS), 0)
    cols = iota((SETS, SETS), 1)
    by_set = sets[0:SETS, :]
    by_set_t = jnp.transpose(by_set)
    fresh = jnp.zeros((SETS, SETS), f32)
    for m in range(KCHIP):
        col = by_set[:, m:m + 1]
        prev = jnp.full((SETS, SETS), -1, i32)
        for k in range(KCHIP):
            prev = jnp.where((by_set_t[k:k + 1, :] == col) & (cols < rows), jnp.maximum(prev, cols), prev)
        prev = jnp.max(prev.astype(f32), axis=1, keepdims=True)
        fresh = fresh + jnp.where((prev < cols.astype(f32)) & (col >= 0) & (rows >= cols), 1.0, 0.0)
    upto = (cols <= rows).astype(f32).astype(jnp.bfloat16)
    distinct = jnp.dot(upto, fresh.astype(jnp.bfloat16), preferred_element_type=f32)
    in_reach = (rows >= cols) & (rows < cols + NXY)
    after = [
        jnp.sum(jnp.where(in_reach & (distinct <= k), 1.0, 0.0), axis=0, keepdims=True) for k in KPLANES
    ]
    to_smem(jnp.concatenate(after, axis=0).astype(i32) + iota((len(KPLANES), SETS), 1), buf_smem)
    starts = [0] * (NZ + 1)
    ok = i32(0)
    for k in reversed(range(len(KPLANES))):
        mine = [0, buf_smem[k, 0]]
        for _ in range(NZ - 1):
            s = mine[-1]
            mine.append(jnp.where(s < SETS, buf_smem[k, jnp.minimum(s, SETS - 1)], SETS))
        enough = (last == n) & (mine[NZ] >= real)
        ok = jnp.where(enough, k + 1, ok)
        starts = [0] + [jnp.where(enough, new, old) for new, old in zip(mine[1:], starts[1:])]
    ok_smem[0] = ok
    for p in range(NZ):
        part = sets[pl.ds(starts[p], NXY), :]
        chips[p * NXY:(p + 1) * NXY, :] = jnp.where(
            iota((NXY, 128), 0) + starts[p] < starts[p + 1], part, blank
        )

    by_chip = chips[...]
    by_chip_t = jnp.transpose(by_chip)
    plane = (rows >> 4) == (cols >> 4)
    earlier = plane & (rows < cols)
    is_first, ranks = [], []
    total = jnp.zeros((1, SETS), f32)
    for m in range(KCHIP):
        row = by_chip_t[m:m + 1, :]
        seen = jnp.zeros((SETS, SETS), f32)
        for k in range(KCHIP):
            seen = jnp.where((by_chip[:, k:k + 1] == row) & earlier, 1.0, seen)
        seen = jnp.max(seen, axis=0, keepdims=True)
        first = jnp.where((row >= 0) & (seen == 0), 1.0, 0.0)
        is_first.append(first)
        ranks.append(total)
        total = total + first
    before = jnp.dot(
        jnp.broadcast_to(total, (8, SETS)).astype(jnp.bfloat16),
        jnp.where(earlier, 1.0, 0.0).astype(jnp.bfloat16), preferred_element_type=f32,
    )[0:1]
    marks = [jnp.where(f > 0, r + before + 1.0, 0.0) for f, r in zip(is_first, ranks)]
    slot_col = jnp.transpose(jnp.broadcast_to(slot_ref[...].astype(f32), (128, n)))
    block = iota((n, SETS), 0).astype(f32)
    slots = []
    for m in range(KCHIP):
        row = by_chip_t[m:m + 1, :]
        slot = jnp.sum(jnp.where(block == row, slot_col, 0.0), axis=0, keepdims=True)
        slots.append(jnp.where(row >= 0, slot, -1.0))
    pad = [jnp.full((8 - KCHIP, SETS), -1.0, f32)]
    tail = [jnp.zeros((SETS - 16, SETS), f32)]
    both = jnp.transpose(jnp.concatenate(marks + pad + slots + pad + tail, axis=0))
    entry_out[...] = both
    local = []
    for m in range(KCHIP):
        row = by_chip_t[m:m + 1, :]
        where = jnp.zeros((SETS, SETS), f32)
        for k in range(KCHIP):
            where = jnp.where((by_chip[:, k:k + 1] == row) & plane, jnp.maximum(where, both[:, k:k + 1]), where)
        local.append(jnp.maximum(jnp.max(where, axis=0, keepdims=True) - 1.0, 0.0))
    local = jnp.concatenate(local + [jnp.zeros((8 - KCHIP, SETS), f32)], axis=0).astype(i32)
    placed = jnp.zeros((SETS, SETS), f32)
    for m in range(KCHIP):
        placed = placed + jnp.where(both[:, m:m + 1] == cols.astype(f32) + 1.0, both[:, 8 + m:9 + m], 0.0)
    placed = jnp.concatenate(
        [jnp.sum(placed[p * NXY:(p + 1) * NXY], axis=0, keepdims=True) for p in range(NZ)], axis=0
    ).astype(i32)
    slots_out[...] = placed
    to_smem(placed, slots_smem)
    to_smem(local, local_smem)

    x, z, c, y = position()
    chip = z * NXY + x * 4 + y
    mine = chips[pl.ds(chip, 1), :].astype(i32)
    to_smem(mine, chip_smem)
    for e in range(EDGES // NC):
        at = NC * e + c
        live = at < chip_smem[0, 24]
        la = jnp.where(live, chip_smem[0, 8 + at], 0)
        lb = jnp.where(live, chip_smem[0, 16 + at], 0)
        info_smem[e] = live.astype(i32)
        info_smem[4 + e] = la
        info_smem[8 + e] = lb
        info_smem[12 + e] = local_smem[la, chip]
        info_smem[16 + e] = local_smem[lb, chip]


def make_plan(every, block_slot):
    vmem, smem = pl.BlockSpec(memory_space=pltpu.VMEM), pl.BlockSpec(memory_space=pltpu.SMEM)
    i32 = jnp.int32
    shape = jax.ShapeDtypeStruct
    return pl.pallas_call(
        plan_kernel,
        out_shape=(
            shape((NZ, 128), i32), shape((8, 512), i32), shape((8, 512), i32), shape((20,), i32),
            shape((SETS, 128), jnp.float32), shape((1,), i32),
        ),
        in_specs=[vmem, vmem],
        out_specs=(vmem, smem, smem, smem, vmem, smem),
        scratch_shapes=[
            pltpu.VMEM((520, 128), jnp.float32), pltpu.VMEM((SETS + 16, 128), jnp.float32),
            pltpu.VMEM((SETS, 128), jnp.float32), pltpu.VMEM((8, 512), i32), pltpu.SMEM((8, 512), i32),
            pltpu.SMEM((8, 512), i32), pltpu.SemaphoreType.DMA,
        ],
        compiler_params=pltpu.CompilerParams(vmem_limit_bytes=32 << 20),
    )(every, block_slot.reshape(1, -1))


def pack_kernel(slot_ref, slots_ref, cluster_ref, emb_ref, out_ref, ids_ref, raw, sems):
    plane = pl.program_id(0)
    held = out_ref.shape[1]

    @pl.when(plane == 0)
    def _():
        for p in range(NZ):
            def one(n, carry):
                pltpu.make_async_copy(
                    emb_ref.at[:, slot_ref[p, n], :], raw.at[p, n], sems.at[p]
                ).start()
                return carry

            lax.fori_loop(0, held, one, 0, unroll=4)

    hot = lax.broadcasted_iota(jnp.int32, (512, 128), 0) == slots_ref[pl.ds(plane, 1), :]
    ids = jnp.dot(
        cluster_ref[...].astype(jnp.bfloat16), jnp.where(hot, 1.0, 0.0).astype(jnp.bfloat16),
        preferred_element_type=jnp.float32,
    )
    ids_ref[0] = ids.astype(jnp.bfloat16)
    pltpu.make_async_copy(raw.at[plane], raw.at[plane], sems.at[plane]).wait()
    for n in range(0, held, 4):
        rows = raw[plane, n:n + 4]
        scale = lax.rsqrt(jnp.sum(rows * rows, axis=-1, keepdims=True) + jnp.float32(1e-06))
        out_ref[0, n:n + 4] = (rows * scale).astype(jnp.bfloat16)


def pack(embeddings, cluster_ids, slots, slots_smem, held):
    return pl.pallas_call(
        pack_kernel,
        grid=(NZ,),
        in_specs=[
            pl.BlockSpec(memory_space=pltpu.SMEM),
            pl.BlockSpec((NZ, 128), lambda p: (0, 0)),
            pl.BlockSpec((ROWS, 512), lambda p: (0, 0)),
            pl.BlockSpec(memory_space=pl.ANY),
        ],
        out_specs=(
            pl.BlockSpec((1, held, ROWS, 512), lambda p: (p, 0, 0, 0)),
            pl.BlockSpec((1, ROWS, 128), lambda p: (p, 0, 0)),
        ),
        scratch_shapes=[
            pltpu.VMEM((NZ, held, ROWS, 512), jnp.float32),
            pltpu.SemaphoreType.DMA((NZ,)),
        ],
        out_shape=(
            jax.ShapeDtypeStruct((NZ, held, ROWS, 512), jnp.bfloat16),
            jax.ShapeDtypeStruct((NZ, ROWS, 128), jnp.bfloat16),
        ),
        compiler_params=pltpu.CompilerParams(
            dimension_semantics=("arbitrary",), vmem_limit_bytes=32 << 20
        ),
    )(slots_smem, slots, cluster_ids, embeddings)


PIECES = tuple((dz, slice(0, 512)) for dz in (0, 1, 7, 2, 6, 3, 5)) + ((4, slice(0, 256)), (4, slice(256, 512)))
NP = len(PIECES)


def spread_kernel(sel_ref, rows_ref, ids_ref, out_ref, idout_ref, *scratch):
    land = scratch[:NP - 1]
    idland = scratch[NP - 1:NP + 6]
    pick = scratch[NP + 6:2 * NP + 6]
    zsend, zrecv, psend, precv, csend, crecv, isend, irecv, jsend, jrecv, local_sem, bsend, brecv = scratch[2 * NP + 6:]
    x, z, c, y = position()
    greet()

    z_copies = [()]
    for i, (dz, cut) in enumerate(PIECES[1:], 1):
        copies = []
        if cut.start == 0:
            copies.append(send(
                ids_ref.at[(z + dz) % 8], idland[dz - 1], isend.at[dz], irecv.at[dz], (0, 0, dz, 0)
            ))
        copies.append(send(
            rows_ref.at[(z + dz) % 8, :, :, cut], land[i - 1], zsend.at[i], zrecv.at[i], (0, 0, dz, 0)
        ))
        z_copies.append(copies)

    p_copies, l_copies, c_copies = [], [], []

    def plane_send(i):
        dz, cut = PIECES[i]
        for copy in z_copies[i]:
            copy.wait_recv()

        def chip(q, carry):
            for n in range(KCHIP):
                at = sel_ref[n, z * NXY + q]
                pick[i][q, n] = rows_ref[z, at] if i == 0 else land[i - 1][at]
            return carry

        lax.fori_loop(0, NXY, chip, 0)
        id_src = ids_ref.at[z] if i == 0 else idland[dz - 1]
        copies, within = [], []
        for d, (dx, dy) in enumerate(STEPS_XY):
            q = ((x + dx) % 4) * 4 + (y + dy) % 4
            src, dst = pick[i].at[q], out_ref.at[0, :, d, dz, :, cut]
            id_dst = idout_ref.at[0, d, dz]
            if d:
                if cut.start == 0:
                    copies.append(send(id_src, id_dst, jsend.at[dz, d], jrecv.at[dz, d], (dx, dy, 0, 0)))
                copies.append(send(src, dst, psend.at[i, d], precv.at[i, d], (dx, dy, 0, 0)))
                continue
            if cut.start == 0:
                within.append(pltpu.make_async_copy(id_src, id_dst, local_sem.at[i, 1]))
            within.append(pltpu.make_async_copy(src, dst, local_sem.at[i, 0]))
        for copy in within:
            copy.start()
        p_copies.append(copies)
        l_copies.append(within)

    def core_send(i):
        dz, cut = PIECES[i]
        for copy in p_copies[i]:
            copy.wait_recv()
        for copy in l_copies[i]:
            copy.wait()
        copies = [send(
            out_ref.at[0, :, :, dz, :, cut], out_ref.at[1, :, :, dz, :, cut], csend.at[i], crecv.at[i], (0, 0, 0, 1)
        )]
        if cut.start == 0:
            copies.append(send(
                idout_ref.at[0, :, dz], idout_ref.at[1, :, dz], bsend.at[dz], brecv.at[dz], (0, 0, 0, 1)
            ))
        c_copies.append(copies)

    for i in range(NP):
        plane_send(i)
        if i >= 2:
            core_send(i - 2)
    core_send(NP - 2)
    core_send(NP - 1)
    for i in range(NP):
        for copy in c_copies[i]:
            copy.wait()
        for copy in p_copies[i]:
            copy.wait_send()
        for copy in z_copies[i]:
            copy.wait_send()


def spread(sel, rows, ids, collective_id):
    dma = pltpu.SemaphoreType.DMA
    held = rows.shape[1]
    wide = [cut.stop - cut.start for _, cut in PIECES]
    return pl.pallas_call(
        spread_kernel,
        out_shape=(
            jax.ShapeDtypeStruct((NC, KCHIP, NXY, NZ, ROWS, 512), jnp.bfloat16),
            jax.ShapeDtypeStruct((NC, NXY, NZ, ROWS, 128), jnp.bfloat16),
        ),
        in_specs=[
            pl.BlockSpec(memory_space=pltpu.SMEM),
            pl.BlockSpec(memory_space=pltpu.VMEM),
            pl.BlockSpec(memory_space=pltpu.VMEM),
        ],
        out_specs=(pl.BlockSpec(memory_space=pl.ANY), pl.BlockSpec(memory_space=pl.ANY)),
        scratch_shapes=[pltpu.VMEM((held, ROWS, w), jnp.bfloat16) for w in wide[1:]]
        + [pltpu.VMEM((ROWS, 128), jnp.bfloat16)] * 7
        + [pltpu.VMEM((NXY, KCHIP, ROWS, w), jnp.bfloat16) for w in wide]
        + [
            dma((NP,)), dma((NP,)), dma((NP, NXY)), dma((NP, NXY)), dma((NP,)), dma((NP,)),
            dma((NZ,)), dma((NZ,)), dma((NZ, NXY)), dma((NZ, NXY)), dma((NP, 2)), dma((NZ,)), dma((NZ,)),
        ],
        compiler_params=pltpu.CompilerParams(
            collective_id=collective_id, has_side_effects=True, vmem_limit_bytes=48 << 20
        ),
    )(sel, rows, ids)


TILE_I, TILE_J = 256, 512


def maxima_kernel(info_ref, left_ref, right_ref, ids_ref, best_ref, id_col, id_row, col_max):
    e = pl.program_id(0)
    length = 2048

    @pl.when(e == 0)
    def _():
        best_ref[...] = jnp.full((8, length), -1.0, jnp.float32)

    @pl.when(info_ref[e] > 0)
    def _():
        la, lb = info_ref[4 + e], info_ref[8 + e]
        ka, kb = info_ref[12 + e], info_ref[16 + e]
        same = (la == lb).astype(jnp.int32)
        lane = lax.broadcasted_iota(jnp.int32, (length, 128), 1)
        ids = ids_ref[...]
        picked = jnp.where(lane == ka, ids.astype(jnp.float32), 0.0)
        id_col[...] = jnp.sum(picked, axis=1, keepdims=True)
        hot = (lax.broadcasted_iota(jnp.int32, (8, 128), 1) == kb).astype(jnp.bfloat16)
        id_row[...] = lax.dot_general(hot, ids, (((1,), (1,)), ((), ())), preferred_element_type=jnp.float32)
        col_max[...] = jnp.full((8, length), -1.0, jnp.float32)
        for i in range(length // TILE_I):
            half, at = divmod(i * TILE_I, length // 2)
            piece = left_ref[half, 0, at:at + TILE_I, :]
            ida = id_col[i * TILE_I:(i + 1) * TILE_I, :]
            row_max = jnp.full((TILE_I, 128), -1.0, jnp.float32)
            for j in range(length // TILE_J):
                half_j, at_j = divmod(j * TILE_J, length // 2)
                other = right_ref[half_j, 0, at_j:at_j + TILE_J, :]
                gram = lax.dot_general(
                    piece, other, (((1,), (1,)), ((), ())), preferred_element_type=jnp.float32
                )
                keep = ida == id_row[0:1, j * TILE_J:(j + 1) * TILE_J]
                masked = jnp.where(keep, gram, -1.0)
                if i * TILE_I // TILE_J == j:
                    rows = lax.broadcasted_iota(jnp.int32, (TILE_I, TILE_J), 0) + i * TILE_I
                    cols = lax.broadcasted_iota(jnp.int32, (TILE_I, TILE_J), 1) + j * TILE_J
                    masked = jnp.where((rows == cols) & (same == 1), -1.0, masked)
                for g in range(TILE_J // 128):
                    row_max = jnp.maximum(row_max, masked[:, g * 128:(g + 1) * 128])
                span = slice(j * TILE_J, (j + 1) * TILE_J)
                col_max[:, span] = jnp.maximum(
                    col_max[:, span], jnp.max(masked.reshape(TILE_I // 8, 8, TILE_J), axis=0)
                )
            across = jnp.max(jnp.transpose(row_max), axis=0, keepdims=True)
            span = slice(i * TILE_I, (i + 1) * TILE_I)
            best_ref[pl.ds(la, 1), span] = jnp.maximum(best_ref[pl.ds(la, 1), span], across)
        down = jnp.max(col_max[...], axis=0, keepdims=True)
        best_ref[pl.ds(lb, 1), :] = jnp.maximum(best_ref[pl.ds(lb, 1), :], down)


def maxima(info, blocks, ids):
    block = (NC, 1, 1024, 512)
    return pl.pallas_call(
        maxima_kernel,
        grid_spec=pltpu.PrefetchScalarGridSpec(
            num_scalar_prefetch=1,
            grid=(EDGES // NC,),
            in_specs=[
                pl.BlockSpec(block, lambda e, s: (0, s[4 + e], 0, 0)),
                pl.BlockSpec(block, lambda e, s: (0, s[8 + e], 0, 0)),
                pl.BlockSpec((2048, 128), lambda e, s: (0, 0)),
            ],
            out_specs=pl.BlockSpec((8, 2048), lambda e, s: (0, 0)),
            scratch_shapes=[
                pltpu.VMEM((2048, 1), jnp.float32),
                pltpu.VMEM((8, 2048), jnp.float32),
                pltpu.VMEM((8, 2048), jnp.float32),
            ],
        ),
        out_shape=jax.ShapeDtypeStruct((8, 2048), jnp.float32),
        compiler_params=pltpu.CompilerParams(
            dimension_semantics=("arbitrary",), vmem_limit_bytes=60 << 20
        ),
    )(info, blocks, blocks, ids)


def return_kernel(best_ref, out_ref, other, merged, stage, land, table, turned, tiles, csend, crecv, psend, precv, zsend, zrecv):
    x, z, c, y = position()
    greet()
    half = SETS * ROWS
    send(best_ref.at[:, half:], other, csend, crecv, (0, 0, 0, 1)).wait()
    merged[...] = jnp.maximum(best_ref[:, :half], other[...])
    stage[...] = jnp.zeros((NXY, 8, 128), jnp.float32)
    for d in range(NXY):
        stage[d, :, 0:64] = merged[:, d * 64:(d + 1) * 64]
    copies = [
        send(stage.at[d], land.at[d], psend.at[d], precv.at[d], (-dx, -dy, 0, 0))
        for d, (dx, dy) in enumerate(STEPS_XY) if d
    ]
    table[:, x * 4 + y, :] = stage[0]
    for copy in copies:
        copy.wait()
    for d, (dx, dy) in enumerate(STEPS_XY):
        if d:
            table[:, ((x + dx) % 4) * 4 + (y + dy) % 4, :] = land[d]
    turned[...] = jnp.transpose(table[...].reshape(8 * NXY, 128))
    copies = [
        send(turned.at[pl.ds(dz * 8, 8)], tiles.at[dz], zsend.at[dz], zrecv.at[dz], (0, 0, -dz, 0))
        for dz in range(1, NZ)
    ]
    out_ref[z] = turned[0:8, :]
    for copy in copies:
        copy.wait()
    for dz in range(1, NZ):
        out_ref[(z + dz) % 8] = tiles[dz]


def give_back(best, collective_id):
    dma = pltpu.SemaphoreType.DMA
    f32 = jnp.float32
    return pl.pallas_call(
        return_kernel,
        out_shape=jax.ShapeDtypeStruct((NZ, ROWS, 128), f32),
        in_specs=[pl.BlockSpec(memory_space=pltpu.VMEM)],
        out_specs=pl.BlockSpec(memory_space=pltpu.VMEM),
        scratch_shapes=[
            pltpu.VMEM((8, SETS * ROWS), f32), pltpu.VMEM((8, SETS * ROWS), f32), pltpu.VMEM((NXY, 8, 128), f32),
            pltpu.VMEM((NXY, 8, 128), f32), pltpu.VMEM((8, NXY, 128), f32), pltpu.VMEM((128, 128), f32),
            pltpu.VMEM((NZ, ROWS, 128), f32),
            dma, dma, dma((NXY,)), dma((NXY,)), dma((NZ,)), dma((NZ,)),
        ],
        compiler_params=pltpu.CompilerParams(collective_id=collective_id, has_side_effects=True, vmem_limit_bytes=16 << 20),
    )(best)


def combine_kernel(got_ref, entry_ref, out_ref):
    count = out_ref.shape[1]
    out = [jnp.full((8, count), -1.0, jnp.float32) for _ in range(ROWS)]
    column = lax.broadcasted_iota(jnp.int32, (128, count), 1).astype(jnp.float32)
    for z in range(NZ):
        values = jnp.transpose(jnp.concatenate([got_ref[z], jnp.zeros((120, 128), jnp.float32)], axis=0))
        slot = jnp.concatenate(
            [entry_ref[z * NXY:(z + 1) * NXY, 8 + n:9 + n] for n in range(8)], axis=0
        )
        match = slot == column
        for r in range(ROWS):
            best = jnp.where(match, values[:, r:r + 1], -1.0)
            out[r] = jnp.maximum(out[r], jnp.max(best.reshape(16, 8, count), axis=0))
    out_ref[...] = jnp.concatenate([jnp.max(o, axis=0, keepdims=True) for o in out], axis=0)


def combine(got, entry, count):
    return pl.pallas_call(
        combine_kernel,
        out_shape=jax.ShapeDtypeStruct((ROWS, count), jnp.float32),
        in_specs=[pl.BlockSpec(memory_space=pltpu.VMEM)] * 2,
        out_specs=pl.BlockSpec(memory_space=pltpu.VMEM),
        compiler_params=pltpu.CompilerParams(vmem_limit_bytes=16 << 20),
    )(got, entry)


def planned(embeddings, cluster_ids, block_slot, plan, size):
    slots, slots_smem, local, info, entry = plan
    rows, ids = pack(embeddings, cluster_ids, slots, slots_smem, KPLANES[size])
    blocks, block_ids = spread(local, rows, ids, 1 + 2 * size)
    best = maxima(info, blocks.reshape(NC, KCHIP, 1024, 512), block_ids.reshape(2048, 128))
    return combine(give_back(best, 2 + 2 * size), entry, block_slot.shape[0])


def body(embeddings, cluster_ids, block_slot, pairs):
    needed = pairs.reshape(-1)
    *plan, ok = make_plan(gather_pairs(needed), block_slot)

    def choose(k):
        if k == len(KPLANES):
            return any_pairs(embeddings, cluster_ids, block_slot, needed)
        return lax.cond(
            ok[0] == k + 1,
            lambda: planned(embeddings, cluster_ids, block_slot, plan, k),
            lambda: choose(k + 1),
        )

    return choose(0)


def solution(mesh):
    return jax.shard_map(
        body,
        mesh=mesh,
        in_specs=(
            P(("store", "grp"), None, None),
            P(("store", "grp"), None),
            P(),
            P(("store", "grp"), None),
        ),
        out_specs=P(("store", "grp"), None),
        check_vma=False,
    )
```

```python
import jax
import jax.numpy as jnp
from jax import lax
from jax.experimental import pallas as pl
from jax.experimental.pallas import tpu as pltpu
from jax.sharding import PartitionSpec as P

MESH = pl.DeviceIdType.MESH
NZ, NXY, NC = 8, 16, 2
KCHIP = 6
EDGES = 6
KPLANES = (56, 60, 64)
SETS = NZ * NXY
ROWS = 8


def pair_maxima(left, right, left_ids, right_ids, same):
    length = left.shape[0]
    step_rows = min(512, length)
    columns = jnp.arange(length)

    def row_block(start):
        piece = lax.dynamic_slice_in_dim(left, start, step_rows, 0)
        piece_ids = lax.dynamic_slice_in_dim(left_ids, start, step_rows, 0)
        gram = lax.dot_general(
            piece, right, (((1,), (1,)), ((), ())), preferred_element_type=jnp.float32
        )
        rows = start + jnp.arange(step_rows)
        keep = (piece_ids[:, None] == right_ids[None, :]) & jnp.logical_not(
            same & (rows[:, None] == columns[None, :])
        )
        masked = jnp.where(keep, gram, jnp.float32(-1.0))
        return (jnp.max(masked, axis=1), jnp.max(masked, axis=0))

    starts = jnp.arange(length // step_rows) * step_rows
    row_best, col_best = lax.map(row_block, starts)
    return (row_best.reshape(length), jnp.max(col_best, axis=0))


def any_pairs(embeddings, cluster_ids, block_slot, needed):
    tile_rows, count, width = embeddings.shape
    n_store = lax.axis_size("store")
    n_grp = lax.axis_size("grp")
    length = tile_rows * n_store * n_grp
    norms = lax.rsqrt(jnp.sum(embeddings * embeddings, axis=-1, keepdims=True) + jnp.float32(1e-06))
    unit = jnp.transpose((embeddings * norms).astype(jnp.bfloat16), (1, 0, 2))
    ids_by_slot = cluster_ids.T
    slots_needed = needed.shape[0]
    every_need = lax.all_gather(needed, ("store", "grp"), axis=0, tiled=True)
    asked = jnp.transpose(every_need.reshape(n_store, n_grp, slots_needed), (2, 0, 1))
    asked_slots = jnp.take(block_slot, asked)
    send_rows = jnp.take(unit, asked_slots, axis=0)
    send_ids = jnp.take(ids_by_slot, asked_slots, axis=0)

    def exchange(rows):
        rows = lax.all_to_all(rows, "store", split_axis=1, concat_axis=1, tiled=True)
        return lax.all_to_all(rows, "grp", split_axis=2, concat_axis=2, tiled=True)

    blocks = exchange(send_rows).reshape(slots_needed, length, width)
    block_ids = exchange(send_ids).reshape(slots_needed, length)
    results = []
    for index in range(slots_needed // 2):
        same = needed[2 * index] == needed[2 * index + 1]
        results += pair_maxima(
            blocks[2 * index], blocks[2 * index + 1], block_ids[2 * index], block_ids[2 * index + 1], same
        )
    maxima = jnp.stack(results, axis=0)
    table = jnp.full((count, length), -1.0, jnp.float32).at[needed].max(maxima)
    table = lax.pmax(table, ("store", "grp"))
    position = lax.axis_index(("store", "grp"))
    mine = lax.dynamic_slice_in_dim(table, position * tile_rows, tile_rows, 1)
    return jnp.zeros((tile_rows, count), jnp.float32).at[:, block_slot].set(mine.T)


def position():
    store, y = lax.axis_index("store"), lax.axis_index("grp")
    return store // 16, (store // 2) % 8, store % 2, y


def stepped(dx, dy, dz, dc):
    x, z, c, y = position()
    return ((((x + dx) % 4) * 8 + (z + dz) % 8) * 2 + (c + dc) % 2, (y + dy) % 4)


STEPS_XY = [(dx, dy) for dx in range(4) for dy in range(4)]


def greet():
    peers = [stepped(0, 0, dz, 0) for dz in range(1, NZ)]
    peers += [stepped(dx, dy, 0, 0) for dx, dy in STEPS_XY[1:]]
    peers += [stepped(0, 0, 0, 1)]
    barrier = pltpu.get_barrier_semaphore()
    for peer in peers:
        pl.semaphore_signal(barrier, inc=1, device_id=peer, device_id_type=MESH)
    pl.semaphore_wait(barrier, len(peers))


def send(src, dst, send_sem, recv_sem, step):
    copy = pltpu.make_async_remote_copy(
        src_ref=src, dst_ref=dst, send_sem=send_sem, recv_sem=recv_sem,
        device_id=stepped(*step), device_id_type=MESH,
    )
    copy.start()
    return copy


def gather_kernel(mine_ref, out_ref, zsend, zrecv, psend, precv, csend, crecv):
    greet()
    out_ref[0, 0, 0] = mine_ref[...]
    copies = [
        send(mine_ref, out_ref.at[0, 0, dz], zsend.at[dz], zrecv.at[dz], (0, 0, dz, 0)) for dz in range(1, NZ)
    ]
    for copy in copies:
        copy.wait()
    copies = [
        send(out_ref.at[0, 0], out_ref.at[0, d], psend.at[d], precv.at[d], (dx, dy, 0, 0))
        for d, (dx, dy) in enumerate(STEPS_XY) if d
    ]
    for copy in copies:
        copy.wait()
    send(out_ref.at[0], out_ref.at[1], csend, crecv, (0, 0, 0, 1)).wait()


def gather_pairs(needed):
    dma = pltpu.SemaphoreType.DMA
    mine = jnp.pad(needed, (0, 128 - needed.shape[0])).reshape(1, 128)
    every = pl.pallas_call(
        gather_kernel,
        out_shape=jax.ShapeDtypeStruct((NC, NXY, NZ, 1, 128), jnp.int32),
        in_specs=[pl.BlockSpec(memory_space=pltpu.VMEM)],
        out_specs=pl.BlockSpec(memory_space=pltpu.VMEM),
        scratch_shapes=[dma((NZ,)), dma((NZ,)), dma((NXY,)), dma((NXY,)), dma, dma],
        compiler_params=pltpu.CompilerParams(collective_id=0, has_side_effects=True),
    )(mine)
    return every.reshape(NC * SETS, 128)


def plan_kernel(
    pairs_ref, slot_ref, slots_out, slots_smem, local_smem, info_smem, entry_out, ok_smem,
    table, sets, chips, buf, buf_smem, chip_smem, sem, outs, out_sems,
):
    n = 512
    f32, i32 = jnp.float32, jnp.int32

    def iota(shape, dim):
        return lax.broadcasted_iota(i32, shape, dim)

    def to_smem(value, ref):
        buf[...] = jnp.zeros((8, n), i32)
        buf[0:value.shape[0], 0:value.shape[1]] = value
        copy = pltpu.make_async_copy(buf, ref, sem)
        copy.start()
        copy.wait()

    got = pairs_ref[...]
    turned = jnp.transpose(got.astype(f32)).astype(i32)
    first_r = jnp.concatenate([turned[0:1], turned[2:3]], axis=1)
    second_r = jnp.concatenate([turned[1:2], turned[3:4]], axis=1)
    first_c = jnp.concatenate([got[:, 0:1], got[:, 2:3]], axis=0)
    second_c = jnp.concatenate([got[:, 1:2], got[:, 3:4]], axis=0)
    key_r, key_c = second_r * n + first_r, second_c * n + first_c
    tie_r, tie_c = key_r * n + iota((1, n), 1), key_c * n + iota((n, 1), 0)
    rank_c = jnp.sum((tie_r < tie_c).astype(f32), axis=1, keepdims=True)
    at = iota((n, n), 1).astype(f32)
    key = jnp.sum(jnp.where(rank_c == at, key_c.astype(f32), 0.0), axis=0, keepdims=True).astype(i32)
    key = jnp.broadcast_to(key, (8, n))
    a, b = key & (n - 1), key >> 9

    lane = iota((8, n), 1)
    sub = iota((8, n), 0)
    nodes = [jnp.full((8, n), -1, i32)] * KCHIP
    count = jnp.zeros((8, n), i32)
    alive = jnp.ones((8, n), i32)
    length = jnp.zeros((8, n), i32)
    left_at = jnp.zeros((8, n), i32)
    right_at = jnp.zeros((8, n), i32)
    for w in range(EDGES):
        aw = a if w == 0 else pltpu.roll(a, n - w, 1)
        bw = b if w == 0 else pltpu.roll(b, n - w, 1)
        at_a = jnp.full((8, n), -1, i32)
        at_b = jnp.full((8, n), -1, i32)
        for m, v in enumerate(nodes):
            at_a = jnp.where(v == aw, m, at_a)
            at_b = jnp.where(v == bw, m, at_b)
        new_a = (at_a < 0).astype(i32)
        new_b = jnp.where((at_b < 0) & (aw != bw), 1, 0)
        la = jnp.where(at_a < 0, count, at_a)
        after = count + new_a
        lb = jnp.where(aw == bw, la, jnp.where(at_b < 0, after, at_b))
        total = after + new_b
        alive = jnp.where((total <= KCHIP) & (lane + w < n), alive, 0)
        put_a, put_b = alive * new_a, alive * new_b
        nodes = [
            jnp.where((put_a == 1) & (la == m), aw, jnp.where((put_b == 1) & (lb == m), bw, v))
            for m, v in enumerate(nodes)
        ]
        count = jnp.where(alive == 1, total, count)
        length = length + alive
        left_at = jnp.where(sub == w, la, left_at)
        right_at = jnp.where(sub == w, lb, right_at)
    held = jnp.full((8, n), -1, i32)
    for m, v in enumerate(nodes):
        held = jnp.where(sub == m, v, held)
    stack = jnp.concatenate([held, left_at, right_at, length], axis=0).astype(f32)
    stack = jnp.concatenate([stack, jnp.zeros((96, n), f32)], axis=0)
    table[0:n, :] = jnp.transpose(stack)
    blank = jnp.where(iota((16, 128), 1) < 8, -1.0, 0.0).astype(f32)
    table[n:n + 8, :] = blank[0:8]
    to_smem(lane + length, buf_smem)

    def one_set(t, carry):
        s, real = carry
        sets[pl.ds(t, 1), :] = table[pl.ds(s, 1), :]
        after = jnp.where(s < n, buf_smem[0, jnp.minimum(s, n - 1)], n)
        return after, real + (s < n).astype(i32)

    last, real = lax.fori_loop(0, SETS, one_set, (i32(0), i32(0)), unroll=4)
    sets[SETS:SETS + 16, :] = blank

    rows = iota((SETS, SETS), 0)
    cols = iota((SETS, SETS), 1)
    by_set = sets[0:SETS, :]
    by_set_t = jnp.transpose(by_set)
    fresh = jnp.zeros((SETS, SETS), f32)
    for m in range(KCHIP):
        col = by_set[:, m:m + 1]
        prev = jnp.full((SETS, SETS), -1, i32)
        for k in range(KCHIP):
            prev = jnp.where((by_set_t[k:k + 1, :] == col) & (cols < rows), jnp.maximum(prev, cols), prev)
        prev = jnp.max(prev.astype(f32), axis=1, keepdims=True)
        fresh = fresh + jnp.where((prev < cols.astype(f32)) & (col >= 0) & (rows >= cols), 1.0, 0.0)
    upto = (cols <= rows).astype(f32).astype(jnp.bfloat16)
    distinct = jnp.dot(upto, fresh.astype(jnp.bfloat16), preferred_element_type=f32)
    in_reach = (rows >= cols) & (rows < cols + NXY)
    after = [
        jnp.sum(jnp.where(in_reach & (distinct <= k), 1.0, 0.0), axis=0, keepdims=True) for k in KPLANES
    ]
    to_smem(jnp.concatenate(after, axis=0).astype(i32) + iota((len(KPLANES), SETS), 1), buf_smem)
    starts = [0] * (NZ + 1)
    ok = i32(0)
    for k in reversed(range(len(KPLANES))):
        mine = [0, buf_smem[k, 0]]
        for _ in range(NZ - 1):
            s = mine[-1]
            mine.append(jnp.where(s < SETS, buf_smem[k, jnp.minimum(s, SETS - 1)], SETS))
        enough = (last == n) & (mine[NZ] >= real)
        ok = jnp.where(enough, k + 1, ok)
        starts = [0] + [jnp.where(enough, new, old) for new, old in zip(mine[1:], starts[1:])]
    ok_smem[0] = ok
    for p in range(NZ):
        part = sets[pl.ds(starts[p], NXY), :]
        chips[p * NXY:(p + 1) * NXY, :] = jnp.where(
            iota((NXY, 128), 0) + starts[p] < starts[p + 1], part, blank
        )

    by_chip = chips[...]
    by_chip_t = jnp.transpose(by_chip)
    plane = (rows >> 4) == (cols >> 4)
    earlier = plane & (rows < cols)
    is_first, ranks = [], []
    total = jnp.zeros((1, SETS), f32)
    for m in range(KCHIP):
        row = by_chip_t[m:m + 1, :]
        seen = jnp.zeros((SETS, SETS), f32)
        for k in range(KCHIP):
            seen = jnp.where((by_chip[:, k:k + 1] == row) & earlier, 1.0, seen)
        seen = jnp.max(seen, axis=0, keepdims=True)
        first = jnp.where((row >= 0) & (seen == 0), 1.0, 0.0)
        is_first.append(first)
        ranks.append(total)
        total = total + first
    before = jnp.dot(
        jnp.broadcast_to(total, (8, SETS)).astype(jnp.bfloat16),
        jnp.where(earlier, 1.0, 0.0).astype(jnp.bfloat16), preferred_element_type=f32,
    )[0:1]
    marks = [jnp.where(f > 0, r + before + 1.0, 0.0) for f, r in zip(is_first, ranks)]
    slot_col = jnp.transpose(jnp.broadcast_to(slot_ref[...].astype(f32), (128, n)))
    block = iota((n, SETS), 0).astype(f32)
    slots = []
    for m in range(KCHIP):
        row = by_chip_t[m:m + 1, :]
        slot = jnp.sum(jnp.where(block == row, slot_col, 0.0), axis=0, keepdims=True)
        slots.append(jnp.where(row >= 0, slot, -1.0))
    pad = [jnp.full((8 - KCHIP, SETS), -1.0, f32)]
    tail = [jnp.zeros((SETS - 16, SETS), f32)]
    both = jnp.transpose(jnp.concatenate(marks + pad + slots + pad + tail, axis=0))
    entry_out[...] = both
    local = []
    for m in range(KCHIP):
        row = by_chip_t[m:m + 1, :]
        where = jnp.zeros((SETS, SETS), f32)
        for k in range(KCHIP):
            where = jnp.where((by_chip[:, k:k + 1] == row) & plane, jnp.maximum(where, both[:, k:k + 1]), where)
        local.append(jnp.maximum(jnp.max(where, axis=0, keepdims=True) - 1.0, 0.0))
    local = jnp.concatenate(local + [jnp.zeros((8 - KCHIP, SETS), f32)], axis=0).astype(i32)
    placed = jnp.zeros((SETS, SETS), f32)
    for m in range(KCHIP):
        placed = placed + jnp.where(both[:, m:m + 1] == cols.astype(f32) + 1.0, both[:, 8 + m:9 + m], 0.0)
    placed = jnp.concatenate(
        [jnp.sum(placed[p * NXY:(p + 1) * NXY], axis=0, keepdims=True) for p in range(NZ)], axis=0
    ).astype(i32)
    slots_out[...] = placed

    x, z, c, y = position()
    chip = z * NXY + x * 4 + y
    mine = chips[pl.ds(chip, 1), :].astype(i32)
    outs[...] = jnp.zeros((3, 8, n), i32)
    copies = []
    for k, (value, ref) in enumerate(((placed, slots_smem), (local, local_smem), (mine, chip_smem))):
        outs[k, 0:value.shape[0], 0:128] = value
        copies.append(pltpu.make_async_copy(outs.at[k], ref, out_sems.at[k]))
    for copy in copies:
        copy.start()
    for copy in copies:
        copy.wait()
    for e in range(EDGES // NC):
        at = NC * e + c
        live = at < chip_smem[0, 24]
        la = jnp.where(live, chip_smem[0, 8 + at], 0)
        lb = jnp.where(live, chip_smem[0, 16 + at], 0)
        info_smem[e] = live.astype(i32)
        info_smem[4 + e] = la
        info_smem[8 + e] = lb
        info_smem[12 + e] = local_smem[la, chip]
        info_smem[16 + e] = local_smem[lb, chip]


def make_plan(every, block_slot):
    vmem, smem = pl.BlockSpec(memory_space=pltpu.VMEM), pl.BlockSpec(memory_space=pltpu.SMEM)
    i32 = jnp.int32
    shape = jax.ShapeDtypeStruct
    return pl.pallas_call(
        plan_kernel,
        out_shape=(
            shape((NZ, 128), i32), shape((8, 512), i32), shape((8, 512), i32), shape((20,), i32),
            shape((SETS, 128), jnp.float32), shape((1,), i32),
        ),
        in_specs=[vmem, vmem],
        out_specs=(vmem, smem, smem, smem, vmem, smem),
        scratch_shapes=[
            pltpu.VMEM((520, 128), jnp.float32), pltpu.VMEM((SETS + 16, 128), jnp.float32),
            pltpu.VMEM((SETS, 128), jnp.float32), pltpu.VMEM((8, 512), i32), pltpu.SMEM((8, 512), i32),
            pltpu.SMEM((8, 512), i32), pltpu.SemaphoreType.DMA, pltpu.VMEM((3, 8, 512), i32),
            pltpu.SemaphoreType.DMA((3,)),
        ],
        compiler_params=pltpu.CompilerParams(vmem_limit_bytes=32 << 20),
    )(every, block_slot.reshape(1, -1))


def pack_kernel(slot_ref, slots_ref, cluster_ref, emb_ref, out_ref, ids_ref, raw, sems):
    plane = pl.program_id(0)
    held = out_ref.shape[1]

    @pl.when(plane == 0)
    def _():
        for p in range(NZ):
            def one(n, carry):
                pltpu.make_async_copy(
                    emb_ref.at[:, slot_ref[p, n], :], raw.at[p, n], sems.at[p]
                ).start()
                return carry

            lax.fori_loop(0, held, one, 0, unroll=4)

    hot = lax.broadcasted_iota(jnp.int32, (512, 128), 0) == slots_ref[pl.ds(plane, 1), :]
    ids = jnp.dot(
        cluster_ref[...].astype(jnp.bfloat16), jnp.where(hot, 1.0, 0.0).astype(jnp.bfloat16),
        preferred_element_type=jnp.float32,
    )
    ids_ref[0] = ids.astype(jnp.bfloat16)
    pltpu.make_async_copy(raw.at[plane], raw.at[plane], sems.at[plane]).wait()
    for n in range(0, held, 4):
        rows = raw[plane, n:n + 4]
        scale = lax.rsqrt(jnp.sum(rows * rows, axis=-1, keepdims=True) + jnp.float32(1e-06))
        out_ref[0, n:n + 4] = (rows * scale).astype(jnp.bfloat16)


def pack(embeddings, cluster_ids, slots, slots_smem, held):
    return pl.pallas_call(
        pack_kernel,
        grid=(NZ,),
        in_specs=[
            pl.BlockSpec(memory_space=pltpu.SMEM),
            pl.BlockSpec((NZ, 128), lambda p: (0, 0)),
            pl.BlockSpec((ROWS, 512), lambda p: (0, 0)),
            pl.BlockSpec(memory_space=pl.ANY),
        ],
        out_specs=(
            pl.BlockSpec((1, held, ROWS, 512), lambda p: (p, 0, 0, 0)),
            pl.BlockSpec((1, ROWS, 128), lambda p: (p, 0, 0)),
        ),
        scratch_shapes=[
            pltpu.VMEM((NZ, held, ROWS, 512), jnp.float32),
            pltpu.SemaphoreType.DMA((NZ,)),
        ],
        out_shape=(
            jax.ShapeDtypeStruct((NZ, held, ROWS, 512), jnp.bfloat16),
            jax.ShapeDtypeStruct((NZ, ROWS, 128), jnp.bfloat16),
        ),
        compiler_params=pltpu.CompilerParams(
            dimension_semantics=("arbitrary",), vmem_limit_bytes=32 << 20
        ),
    )(slots_smem, slots, cluster_ids, embeddings)


PIECES = tuple((dz, slice(0, 512)) for dz in (0, 1, 7, 2, 6, 3, 5)) + ((4, slice(0, 256)), (4, slice(256, 512)))
NP = len(PIECES)


def spread_kernel(sel_ref, rows_ref, ids_ref, out_ref, idout_ref, *scratch):
    land = scratch[:NP - 1]
    idland = scratch[NP - 1:NP + 6]
    pick = scratch[NP + 6:2 * NP + 6]
    zsend, zrecv, psend, precv, csend, crecv, isend, irecv, jsend, jrecv, local_sem, bsend, brecv = scratch[2 * NP + 6:]
    x, z, c, y = position()
    greet()

    z_copies = [()]
    for i, (dz, cut) in enumerate(PIECES[1:], 1):
        copies = []
        if cut.start == 0:
            copies.append(send(
                ids_ref.at[(z + dz) % 8], idland[dz - 1], isend.at[dz], irecv.at[dz], (0, 0, dz, 0)
            ))
        copies.append(send(
            rows_ref.at[(z + dz) % 8, :, :, cut], land[i - 1], zsend.at[i], zrecv.at[i], (0, 0, dz, 0)
        ))
        z_copies.append(copies)

    p_copies, l_copies, c_copies = [], [], []

    def plane_send(i):
        dz, cut = PIECES[i]
        for copy in z_copies[i]:
            copy.wait_recv()

        def chip(q, carry):
            for n in range(KCHIP):
                at = sel_ref[n, z * NXY + q]
                pick[i][q, n] = rows_ref[z, at] if i == 0 else land[i - 1][at]
            return carry

        lax.fori_loop(0, NXY, chip, 0)
        id_src = ids_ref.at[z] if i == 0 else idland[dz - 1]
        copies, within = [], []
        for d, (dx, dy) in enumerate(STEPS_XY):
            q = ((x + dx) % 4) * 4 + (y + dy) % 4
            src, dst = pick[i].at[q], out_ref.at[0, :, d, dz, :, cut]
            id_dst = idout_ref.at[0, d, dz]
            if d:
                if cut.start == 0:
                    copies.append(send(id_src, id_dst, jsend.at[dz, d], jrecv.at[dz, d], (dx, dy, 0, 0)))
                copies.append(send(src, dst, psend.at[i, d], precv.at[i, d], (dx, dy, 0, 0)))
                continue
            if cut.start == 0:
                within.append(pltpu.make_async_copy(id_src, id_dst, local_sem.at[i, 1]))
            within.append(pltpu.make_async_copy(src, dst, local_sem.at[i, 0]))
        for copy in within:
            copy.start()
        p_copies.append(copies)
        l_copies.append(within)

    def core_send(i):
        dz, cut = PIECES[i]
        for copy in p_copies[i]:
            copy.wait_recv()
        for copy in l_copies[i]:
            copy.wait()
        copies = [send(
            out_ref.at[0, :, :, dz, :, cut], out_ref.at[1, :, :, dz, :, cut], csend.at[i], crecv.at[i], (0, 0, 0, 1)
        )]
        if cut.start == 0:
            copies.append(send(
                idout_ref.at[0, :, dz], idout_ref.at[1, :, dz], bsend.at[dz], brecv.at[dz], (0, 0, 0, 1)
            ))
        c_copies.append(copies)

    for i in range(NP):
        plane_send(i)
        if i >= 2:
            core_send(i - 2)
    core_send(NP - 2)
    core_send(NP - 1)
    for i in range(NP):
        for copy in c_copies[i]:
            copy.wait()
        for copy in p_copies[i]:
            copy.wait_send()
        for copy in z_copies[i]:
            copy.wait_send()


def spread(sel, rows, ids, collective_id):
    dma = pltpu.SemaphoreType.DMA
    held = rows.shape[1]
    wide = [cut.stop - cut.start for _, cut in PIECES]
    return pl.pallas_call(
        spread_kernel,
        out_shape=(
            jax.ShapeDtypeStruct((NC, KCHIP, NXY, NZ, ROWS, 512), jnp.bfloat16),
            jax.ShapeDtypeStruct((NC, NXY, NZ, ROWS, 128), jnp.bfloat16),
        ),
        in_specs=[
            pl.BlockSpec(memory_space=pltpu.SMEM),
            pl.BlockSpec(memory_space=pltpu.VMEM),
            pl.BlockSpec(memory_space=pltpu.VMEM),
        ],
        out_specs=(pl.BlockSpec(memory_space=pl.ANY), pl.BlockSpec(memory_space=pl.ANY)),
        scratch_shapes=[pltpu.VMEM((held, ROWS, w), jnp.bfloat16) for w in wide[1:]]
        + [pltpu.VMEM((ROWS, 128), jnp.bfloat16)] * 7
        + [pltpu.VMEM((NXY, KCHIP, ROWS, w), jnp.bfloat16) for w in wide]
        + [
            dma((NP,)), dma((NP,)), dma((NP, NXY)), dma((NP, NXY)), dma((NP,)), dma((NP,)),
            dma((NZ,)), dma((NZ,)), dma((NZ, NXY)), dma((NZ, NXY)), dma((NP, 2)), dma((NZ,)), dma((NZ,)),
        ],
        compiler_params=pltpu.CompilerParams(
            collective_id=collective_id, has_side_effects=True, vmem_limit_bytes=48 << 20
        ),
    )(sel, rows, ids)


TILE_I, TILE_J = 256, 512


def maxima_kernel(info_ref, left_ref, right_ref, ids_ref, best_ref, id_col, id_row, col_max):
    e = pl.program_id(0)
    length = 2048

    @pl.when(e == 0)
    def _():
        best_ref[...] = jnp.full((8, length), -1.0, jnp.float32)

    @pl.when(info_ref[e] > 0)
    def _():
        la, lb = info_ref[4 + e], info_ref[8 + e]
        ka, kb = info_ref[12 + e], info_ref[16 + e]
        same = (la == lb).astype(jnp.int32)
        lane = lax.broadcasted_iota(jnp.int32, (length, 128), 1)
        ids = ids_ref[...]
        picked = jnp.where(lane == ka, ids.astype(jnp.float32), 0.0)
        id_col[...] = jnp.sum(picked, axis=1, keepdims=True)
        hot = (lax.broadcasted_iota(jnp.int32, (8, 128), 1) == kb).astype(jnp.bfloat16)
        id_row[...] = lax.dot_general(hot, ids, (((1,), (1,)), ((), ())), preferred_element_type=jnp.float32)
        col_max[...] = jnp.full((8, length), -1.0, jnp.float32)
        for i in range(length // TILE_I):
            half, at = divmod(i * TILE_I, length // 2)
            piece = left_ref[half, 0, at:at + TILE_I, :]
            ida = id_col[i * TILE_I:(i + 1) * TILE_I, :]
            row_max = jnp.full((TILE_I, 128), -1.0, jnp.float32)
            for j in range(length // TILE_J):
                half_j, at_j = divmod(j * TILE_J, length // 2)
                other = right_ref[half_j, 0, at_j:at_j + TILE_J, :]
                gram = lax.dot_general(
                    piece, other, (((1,), (1,)), ((), ())), preferred_element_type=jnp.float32
                )
                keep = ida == id_row[0:1, j * TILE_J:(j + 1) * TILE_J]
                masked = jnp.where(keep, gram, -1.0)
                if i * TILE_I // TILE_J == j:
                    rows = lax.broadcasted_iota(jnp.int32, (TILE_I, TILE_J), 0) + i * TILE_I
                    cols = lax.broadcasted_iota(jnp.int32, (TILE_I, TILE_J), 1) + j * TILE_J
                    masked = jnp.where((rows == cols) & (same == 1), -1.0, masked)
                for g in range(TILE_J // 128):
                    row_max = jnp.maximum(row_max, masked[:, g * 128:(g + 1) * 128])
                span = slice(j * TILE_J, (j + 1) * TILE_J)
                col_max[:, span] = jnp.maximum(
                    col_max[:, span], jnp.max(masked.reshape(TILE_I // 8, 8, TILE_J), axis=0)
                )
            across = jnp.max(jnp.transpose(row_max), axis=0, keepdims=True)
            span = slice(i * TILE_I, (i + 1) * TILE_I)
            best_ref[pl.ds(la, 1), span] = jnp.maximum(best_ref[pl.ds(la, 1), span], across)
        down = jnp.max(col_max[...], axis=0, keepdims=True)
        best_ref[pl.ds(lb, 1), :] = jnp.maximum(best_ref[pl.ds(lb, 1), :], down)


def maxima(info, blocks, ids):
    block = (NC, 1, 1024, 512)
    return pl.pallas_call(
        maxima_kernel,
        grid_spec=pltpu.PrefetchScalarGridSpec(
            num_scalar_prefetch=1,
            grid=(EDGES // NC,),
            in_specs=[
                pl.BlockSpec(block, lambda e, s: (0, s[4 + e], 0, 0)),
                pl.BlockSpec(block, lambda e, s: (0, s[8 + e], 0, 0)),
                pl.BlockSpec((2048, 128), lambda e, s: (0, 0)),
            ],
            out_specs=pl.BlockSpec((8, 2048), lambda e, s: (0, 0)),
            scratch_shapes=[
                pltpu.VMEM((2048, 1), jnp.float32),
                pltpu.VMEM((8, 2048), jnp.float32),
                pltpu.VMEM((8, 2048), jnp.float32),
            ],
        ),
        out_shape=jax.ShapeDtypeStruct((8, 2048), jnp.float32),
        compiler_params=pltpu.CompilerParams(
            dimension_semantics=("arbitrary",), vmem_limit_bytes=60 << 20
        ),
    )(info, blocks, blocks, ids)


def return_kernel(best_ref, out_ref, other, merged, stage, land, table, turned, tiles, csend, crecv, psend, precv, zsend, zrecv):
    x, z, c, y = position()
    greet()
    half = SETS * ROWS
    send(best_ref.at[:, half:], other, csend, crecv, (0, 0, 0, 1)).wait()
    merged[...] = jnp.maximum(best_ref[:, :half], other[...])
    stage[...] = jnp.zeros((NXY, 8, 128), jnp.float32)
    for d in range(NXY):
        stage[d, :, 0:64] = merged[:, d * 64:(d + 1) * 64]
    copies = [
        send(stage.at[d], land.at[d], psend.at[d], precv.at[d], (-dx, -dy, 0, 0))
        for d, (dx, dy) in enumerate(STEPS_XY) if d
    ]
    table[:, x * 4 + y, :] = stage[0]
    for copy in copies:
        copy.wait()
    for d, (dx, dy) in enumerate(STEPS_XY):
        if d:
            table[:, ((x + dx) % 4) * 4 + (y + dy) % 4, :] = land[d]
    turned[...] = jnp.transpose(table[...].reshape(8 * NXY, 128))
    copies = [
        send(turned.at[pl.ds(dz * 8, 8)], tiles.at[dz], zsend.at[dz], zrecv.at[dz], (0, 0, -dz, 0))
        for dz in range(1, NZ)
    ]
    out_ref[z] = turned[0:8, :]
    for copy in copies:
        copy.wait()
    for dz in range(1, NZ):
        out_ref[(z + dz) % 8] = tiles[dz]


def give_back(best, collective_id):
    dma = pltpu.SemaphoreType.DMA
    f32 = jnp.float32
    return pl.pallas_call(
        return_kernel,
        out_shape=jax.ShapeDtypeStruct((NZ, ROWS, 128), f32),
        in_specs=[pl.BlockSpec(memory_space=pltpu.VMEM)],
        out_specs=pl.BlockSpec(memory_space=pltpu.VMEM),
        scratch_shapes=[
            pltpu.VMEM((8, SETS * ROWS), f32), pltpu.VMEM((8, SETS * ROWS), f32), pltpu.VMEM((NXY, 8, 128), f32),
            pltpu.VMEM((NXY, 8, 128), f32), pltpu.VMEM((8, NXY, 128), f32), pltpu.VMEM((128, 128), f32),
            pltpu.VMEM((NZ, ROWS, 128), f32),
            dma, dma, dma((NXY,)), dma((NXY,)), dma((NZ,)), dma((NZ,)),
        ],
        compiler_params=pltpu.CompilerParams(collective_id=collective_id, has_side_effects=True, vmem_limit_bytes=16 << 20),
    )(best)


def combine_kernel(got_ref, entry_ref, out_ref):
    count = out_ref.shape[1]
    out = [jnp.full((8, count), -1.0, jnp.float32) for _ in range(ROWS)]
    column = lax.broadcasted_iota(jnp.int32, (128, count), 1).astype(jnp.float32)
    for z in range(NZ):
        values = jnp.transpose(jnp.concatenate([got_ref[z], jnp.zeros((120, 128), jnp.float32)], axis=0))
        slot = jnp.concatenate(
            [entry_ref[z * NXY:(z + 1) * NXY, 8 + n:9 + n] for n in range(8)], axis=0
        )
        match = slot == column
        for r in range(ROWS):
            best = jnp.where(match, values[:, r:r + 1], -1.0)
            out[r] = jnp.maximum(out[r], jnp.max(best.reshape(16, 8, count), axis=0))
    out_ref[...] = jnp.concatenate([jnp.max(o, axis=0, keepdims=True) for o in out], axis=0)


def combine(got, entry, count):
    return pl.pallas_call(
        combine_kernel,
        out_shape=jax.ShapeDtypeStruct((ROWS, count), jnp.float32),
        in_specs=[pl.BlockSpec(memory_space=pltpu.VMEM)] * 2,
        out_specs=pl.BlockSpec(memory_space=pltpu.VMEM),
        compiler_params=pltpu.CompilerParams(vmem_limit_bytes=16 << 20),
    )(got, entry)


def planned(embeddings, cluster_ids, block_slot, plan, size):
    slots, slots_smem, local, info, entry = plan
    rows, ids = pack(embeddings, cluster_ids, slots, slots_smem, KPLANES[size])
    blocks, block_ids = spread(local, rows, ids, 1 + 2 * size)
    best = maxima(info, blocks.reshape(NC, KCHIP, 1024, 512), block_ids.reshape(2048, 128))
    return combine(give_back(best, 2 + 2 * size), entry, block_slot.shape[0])


def body(embeddings, cluster_ids, block_slot, pairs):
    needed = pairs.reshape(-1)
    *plan, ok = make_plan(gather_pairs(needed), block_slot)

    def choose(k):
        if k == len(KPLANES):
            return any_pairs(embeddings, cluster_ids, block_slot, needed)
        return lax.cond(
            ok[0] == k + 1,
            lambda: planned(embeddings, cluster_ids, block_slot, plan, k),
            lambda: choose(k + 1),
        )

    return choose(0)


def solution(mesh):
    return jax.shard_map(
        body,
        mesh=mesh,
        in_specs=(
            P(("store", "grp"), None, None),
            P(("store", "grp"), None),
            P(),
            P(("store", "grp"), None),
        ),
        out_specs=P(("store", "grp"), None),
        check_vma=False,
    )
```

```python
import jax
import jax.numpy as jnp
from jax import lax
from jax.experimental import pallas as pl
from jax.experimental.pallas import tpu as pltpu
from jax.sharding import PartitionSpec as P

MESH = pl.DeviceIdType.MESH
NZ, NXY, NC = 8, 16, 2
KCHIP = 6
EDGES = 6
KPLANES = (60, 64)
SETS = NZ * NXY
ROWS = 8


def pair_maxima(left, right, left_ids, right_ids, same):
    length = left.shape[0]
    step_rows = min(512, length)
    columns = jnp.arange(length)

    def row_block(start):
        piece = lax.dynamic_slice_in_dim(left, start, step_rows, 0)
        piece_ids = lax.dynamic_slice_in_dim(left_ids, start, step_rows, 0)
        gram = lax.dot_general(
            piece, right, (((1,), (1,)), ((), ())), preferred_element_type=jnp.float32
        )
        rows = start + jnp.arange(step_rows)
        keep = (piece_ids[:, None] == right_ids[None, :]) & jnp.logical_not(
            same & (rows[:, None] == columns[None, :])
        )
        masked = jnp.where(keep, gram, jnp.float32(-1.0))
        return (jnp.max(masked, axis=1), jnp.max(masked, axis=0))

    starts = jnp.arange(length // step_rows) * step_rows
    row_best, col_best = lax.map(row_block, starts)
    return (row_best.reshape(length), jnp.max(col_best, axis=0))


def any_pairs(embeddings, cluster_ids, block_slot, needed):
    tile_rows, count, width = embeddings.shape
    n_store = lax.axis_size("store")
    n_grp = lax.axis_size("grp")
    length = tile_rows * n_store * n_grp
    norms = lax.rsqrt(jnp.sum(embeddings * embeddings, axis=-1, keepdims=True) + jnp.float32(1e-06))
    unit = jnp.transpose((embeddings * norms).astype(jnp.bfloat16), (1, 0, 2))
    ids_by_slot = cluster_ids.T
    slots_needed = needed.shape[0]
    every_need = lax.all_gather(needed, ("store", "grp"), axis=0, tiled=True)
    asked = jnp.transpose(every_need.reshape(n_store, n_grp, slots_needed), (2, 0, 1))
    asked_slots = jnp.take(block_slot, asked)
    send_rows = jnp.take(unit, asked_slots, axis=0)
    send_ids = jnp.take(ids_by_slot, asked_slots, axis=0)

    def exchange(rows):
        rows = lax.all_to_all(rows, "store", split_axis=1, concat_axis=1, tiled=True)
        return lax.all_to_all(rows, "grp", split_axis=2, concat_axis=2, tiled=True)

    blocks = exchange(send_rows).reshape(slots_needed, length, width)
    block_ids = exchange(send_ids).reshape(slots_needed, length)
    results = []
    for index in range(slots_needed // 2):
        same = needed[2 * index] == needed[2 * index + 1]
        results += pair_maxima(
            blocks[2 * index], blocks[2 * index + 1], block_ids[2 * index], block_ids[2 * index + 1], same
        )
    maxima = jnp.stack(results, axis=0)
    table = jnp.full((count, length), -1.0, jnp.float32).at[needed].max(maxima)
    table = lax.pmax(table, ("store", "grp"))
    position = lax.axis_index(("store", "grp"))
    mine = lax.dynamic_slice_in_dim(table, position * tile_rows, tile_rows, 1)
    return jnp.zeros((tile_rows, count), jnp.float32).at[:, block_slot].set(mine.T)


def position():
    store, y = lax.axis_index("store"), lax.axis_index("grp")
    return store // 16, (store // 2) % 8, store % 2, y


def stepped(dx, dy, dz, dc):
    x, z, c, y = position()
    return ((((x + dx) % 4) * 8 + (z + dz) % 8) * 2 + (c + dc) % 2, (y + dy) % 4)


STEPS_XY = [(dx, dy) for dx in range(4) for dy in range(4)]


def greet():
    peers = [stepped(0, 0, dz, 0) for dz in range(1, NZ)]
    peers += [stepped(dx, dy, 0, 0) for dx, dy in STEPS_XY[1:]]
    peers += [stepped(0, 0, 0, 1)]
    barrier = pltpu.get_barrier_semaphore()
    for peer in peers:
        pl.semaphore_signal(barrier, inc=1, device_id=peer, device_id_type=MESH)
    pl.semaphore_wait(barrier, len(peers))


def send(src, dst, send_sem, recv_sem, step):
    copy = pltpu.make_async_remote_copy(
        src_ref=src, dst_ref=dst, send_sem=send_sem, recv_sem=recv_sem,
        device_id=stepped(*step), device_id_type=MESH,
    )
    copy.start()
    return copy


def gather_kernel(mine_ref, out_ref, zsend, zrecv, psend, precv, csend, crecv):
    greet()
    out_ref[0, 0, 0] = mine_ref[...]
    copies = [
        send(mine_ref, out_ref.at[0, 0, dz], zsend.at[dz], zrecv.at[dz], (0, 0, dz, 0)) for dz in range(1, NZ)
    ]
    for copy in copies:
        copy.wait()
    copies = [
        send(out_ref.at[0, 0], out_ref.at[0, d], psend.at[d], precv.at[d], (dx, dy, 0, 0))
        for d, (dx, dy) in enumerate(STEPS_XY) if d
    ]
    for copy in copies:
        copy.wait()
    send(out_ref.at[0], out_ref.at[1], csend, crecv, (0, 0, 0, 1)).wait()


def gather_pairs(needed):
    dma = pltpu.SemaphoreType.DMA
    mine = jnp.pad(needed, (0, 128 - needed.shape[0])).reshape(1, 128)
    every = pl.pallas_call(
        gather_kernel,
        out_shape=jax.ShapeDtypeStruct((NC, NXY, NZ, 1, 128), jnp.int32),
        in_specs=[pl.BlockSpec(memory_space=pltpu.VMEM)],
        out_specs=pl.BlockSpec(memory_space=pltpu.VMEM),
        scratch_shapes=[dma((NZ,)), dma((NZ,)), dma((NXY,)), dma((NXY,)), dma, dma],
        compiler_params=pltpu.CompilerParams(collective_id=0, has_side_effects=True),
    )(mine)
    return every.reshape(NC * SETS, 128)


def plan_kernel(
    pairs_ref, slot_ref, slots_out, slots_smem, local_smem, info_smem, entry_out, ok_smem,
    table, sets, chips, buf, buf_smem, chip_smem, sem, outs, out_sems,
):
    n = 512
    f32, i32 = jnp.float32, jnp.int32

    def iota(shape, dim):
        return lax.broadcasted_iota(i32, shape, dim)

    def to_smem(value, ref):
        buf[...] = jnp.zeros((8, n), i32)
        buf[0:value.shape[0], 0:value.shape[1]] = value
        copy = pltpu.make_async_copy(buf, ref, sem)
        copy.start()
        copy.wait()

    got = pairs_ref[...]
    turned = jnp.transpose(got.astype(f32)).astype(i32)
    first_r = jnp.concatenate([turned[0:1], turned[2:3]], axis=1)
    second_r = jnp.concatenate([turned[1:2], turned[3:4]], axis=1)
    first_c = jnp.concatenate([got[:, 0:1], got[:, 2:3]], axis=0)
    second_c = jnp.concatenate([got[:, 1:2], got[:, 3:4]], axis=0)
    key_r, key_c = second_r * n + first_r, second_c * n + first_c
    tie_r, tie_c = key_r * n + iota((1, n), 1), key_c * n + iota((n, 1), 0)
    rank_c = jnp.sum((tie_r < tie_c).astype(f32), axis=1, keepdims=True)
    at = iota((n, n), 1).astype(f32)
    key = jnp.sum(jnp.where(rank_c == at, key_c.astype(f32), 0.0), axis=0, keepdims=True).astype(i32)
    key = jnp.broadcast_to(key, (8, n))
    a, b = key & (n - 1), key >> 9

    lane = iota((8, n), 1)
    sub = iota((8, n), 0)
    nodes = [jnp.full((8, n), -1, i32)] * KCHIP
    count = jnp.zeros((8, n), i32)
    alive = jnp.ones((8, n), i32)
    length = jnp.zeros((8, n), i32)
    left_at = jnp.zeros((8, n), i32)
    right_at = jnp.zeros((8, n), i32)
    for w in range(EDGES):
        aw = a if w == 0 else pltpu.roll(a, n - w, 1)
        bw = b if w == 0 else pltpu.roll(b, n - w, 1)
        at_a = jnp.full((8, n), -1, i32)
        at_b = jnp.full((8, n), -1, i32)
        for m, v in enumerate(nodes):
            at_a = jnp.where(v == aw, m, at_a)
            at_b = jnp.where(v == bw, m, at_b)
        new_a = (at_a < 0).astype(i32)
        new_b = jnp.where((at_b < 0) & (aw != bw), 1, 0)
        la = jnp.where(at_a < 0, count, at_a)
        after = count + new_a
        lb = jnp.where(aw == bw, la, jnp.where(at_b < 0, after, at_b))
        total = after + new_b
        alive = jnp.where((total <= KCHIP) & (lane + w < n), alive, 0)
        put_a, put_b = alive * new_a, alive * new_b
        nodes = [
            jnp.where((put_a == 1) & (la == m), aw, jnp.where((put_b == 1) & (lb == m), bw, v))
            for m, v in enumerate(nodes)
        ]
        count = jnp.where(alive == 1, total, count)
        length = length + alive
        left_at = jnp.where(sub == w, la, left_at)
        right_at = jnp.where(sub == w, lb, right_at)
    held = jnp.full((8, n), -1, i32)
    for m, v in enumerate(nodes):
        held = jnp.where(sub == m, v, held)
    stack = jnp.concatenate([held, left_at, right_at, length], axis=0).astype(f32)
    stack = jnp.concatenate([stack, jnp.zeros((96, n), f32)], axis=0)
    table[0:n, :] = jnp.transpose(stack)
    blank = jnp.where(iota((16, 128), 1) < 8, -1.0, 0.0).astype(f32)
    table[n:n + 8, :] = blank[0:8]
    to_smem(lane + length, buf_smem)

    def one_set(t, carry):
        s, real = carry
        sets[pl.ds(t, 1), :] = table[pl.ds(s, 1), :]
        after = jnp.where(s < n, buf_smem[0, jnp.minimum(s, n - 1)], n)
        return after, real + (s < n).astype(i32)

    last, real = lax.fori_loop(0, SETS, one_set, (i32(0), i32(0)), unroll=4)
    sets[SETS:SETS + 16, :] = blank

    rows = iota((SETS, SETS), 0)
    cols = iota((SETS, SETS), 1)
    by_set = sets[0:SETS, :]
    by_set_t = jnp.transpose(by_set)
    fresh = jnp.zeros((SETS, SETS), f32)
    for m in range(KCHIP):
        col = by_set[:, m:m + 1]
        prev = jnp.full((SETS, SETS), -1, i32)
        for k in range(KCHIP):
            prev = jnp.where((by_set_t[k:k + 1, :] == col) & (cols < rows), jnp.maximum(prev, cols), prev)
        prev = jnp.max(prev.astype(f32), axis=1, keepdims=True)
        fresh = fresh + jnp.where((prev < cols.astype(f32)) & (col >= 0) & (rows >= cols), 1.0, 0.0)
    upto = (cols <= rows).astype(f32).astype(jnp.bfloat16)
    distinct = jnp.dot(upto, fresh.astype(jnp.bfloat16), preferred_element_type=f32)
    in_reach = (rows >= cols) & (rows < cols + NXY)
    after = [
        jnp.sum(jnp.where(in_reach & (distinct <= k), 1.0, 0.0), axis=0, keepdims=True) for k in KPLANES
    ]
    to_smem(jnp.concatenate(after, axis=0).astype(i32) + iota((len(KPLANES), SETS), 1), buf_smem)
    starts = [0] * (NZ + 1)
    ok = i32(0)
    for k in reversed(range(len(KPLANES))):
        mine = [0, buf_smem[k, 0]]
        for _ in range(NZ - 1):
            s = mine[-1]
            mine.append(jnp.where(s < SETS, buf_smem[k, jnp.minimum(s, SETS - 1)], SETS))
        enough = (last == n) & (mine[NZ] >= real)
        ok = jnp.where(enough, k + 1, ok)
        starts = [0] + [jnp.where(enough, new, old) for new, old in zip(mine[1:], starts[1:])]
    ok_smem[0] = ok
    for p in range(NZ):
        part = sets[pl.ds(starts[p], NXY), :]
        chips[p * NXY:(p + 1) * NXY, :] = jnp.where(
            iota((NXY, 128), 0) + starts[p] < starts[p + 1], part, blank
        )

    by_chip = chips[...]
    by_chip_t = jnp.transpose(by_chip)
    plane = (rows >> 4) == (cols >> 4)
    earlier = plane & (rows < cols)
    is_first, ranks = [], []
    total = jnp.zeros((1, SETS), f32)
    for m in range(KCHIP):
        row = by_chip_t[m:m + 1, :]
        seen = jnp.zeros((SETS, SETS), f32)
        for k in range(KCHIP):
            seen = jnp.where((by_chip[:, k:k + 1] == row) & earlier, 1.0, seen)
        seen = jnp.max(seen, axis=0, keepdims=True)
        first = jnp.where((row >= 0) & (seen == 0), 1.0, 0.0)
        is_first.append(first)
        ranks.append(total)
        total = total + first
    before = jnp.dot(
        jnp.broadcast_to(total, (8, SETS)).astype(jnp.bfloat16),
        jnp.where(earlier, 1.0, 0.0).astype(jnp.bfloat16), preferred_element_type=f32,
    )[0:1]
    marks = [jnp.where(f > 0, r + before + 1.0, 0.0) for f, r in zip(is_first, ranks)]
    slot_col = jnp.transpose(jnp.broadcast_to(slot_ref[...].astype(f32), (128, n)))
    block = iota((n, SETS), 0).astype(f32)
    slots = []
    for m in range(KCHIP):
        row = by_chip_t[m:m + 1, :]
        slot = jnp.sum(jnp.where(block == row, slot_col, 0.0), axis=0, keepdims=True)
        slots.append(jnp.where(row >= 0, slot, -1.0))
    pad = [jnp.full((8 - KCHIP, SETS), -1.0, f32)]
    tail = [jnp.zeros((SETS - 16, SETS), f32)]
    both = jnp.transpose(jnp.concatenate(marks + pad + slots + pad + tail, axis=0))
    entry_out[...] = both
    local = []
    for m in range(KCHIP):
        row = by_chip_t[m:m + 1, :]
        where = jnp.zeros((SETS, SETS), f32)
        for k in range(KCHIP):
            where = jnp.where((by_chip[:, k:k + 1] == row) & plane, jnp.maximum(where, both[:, k:k + 1]), where)
        local.append(jnp.maximum(jnp.max(where, axis=0, keepdims=True) - 1.0, 0.0))
    local = jnp.concatenate(local + [jnp.zeros((8 - KCHIP, SETS), f32)], axis=0).astype(i32)
    placed = jnp.zeros((SETS, SETS), f32)
    for m in range(KCHIP):
        placed = placed + jnp.where(both[:, m:m + 1] == cols.astype(f32) + 1.0, both[:, 8 + m:9 + m], 0.0)
    placed = jnp.concatenate(
        [jnp.sum(placed[p * NXY:(p + 1) * NXY], axis=0, keepdims=True) for p in range(NZ)], axis=0
    ).astype(i32)
    slots_out[...] = placed

    x, z, c, y = position()
    chip = z * NXY + x * 4 + y
    mine = chips[pl.ds(chip, 1), :].astype(i32)
    outs[...] = jnp.zeros((3, 8, n), i32)
    copies = []
    for k, (value, ref) in enumerate(((placed, slots_smem), (local, local_smem), (mine, chip_smem))):
        outs[k, 0:value.shape[0], 0:128] = value
        copies.append(pltpu.make_async_copy(outs.at[k], ref, out_sems.at[k]))
    for copy in copies:
        copy.start()
    for copy in copies:
        copy.wait()
    for e in range(EDGES // NC):
        at = NC * e + c
        live = at < chip_smem[0, 24]
        la = jnp.where(live, chip_smem[0, 8 + at], 0)
        lb = jnp.where(live, chip_smem[0, 16 + at], 0)
        info_smem[e] = live.astype(i32)
        info_smem[4 + e] = la
        info_smem[8 + e] = lb
        info_smem[12 + e] = local_smem[la, chip]
        info_smem[16 + e] = local_smem[lb, chip]


def make_plan(every, block_slot):
    vmem, smem = pl.BlockSpec(memory_space=pltpu.VMEM), pl.BlockSpec(memory_space=pltpu.SMEM)
    i32 = jnp.int32
    shape = jax.ShapeDtypeStruct
    return pl.pallas_call(
        plan_kernel,
        out_shape=(
            shape((NZ, 128), i32), shape((8, 512), i32), shape((8, 512), i32), shape((20,), i32),
            shape((SETS, 128), jnp.float32), shape((1,), i32),
        ),
        in_specs=[vmem, vmem],
        out_specs=(vmem, smem, smem, smem, vmem, smem),
        scratch_shapes=[
            pltpu.VMEM((520, 128), jnp.float32), pltpu.VMEM((SETS + 16, 128), jnp.float32),
            pltpu.VMEM((SETS, 128), jnp.float32), pltpu.VMEM((8, 512), i32), pltpu.SMEM((8, 512), i32),
            pltpu.SMEM((8, 512), i32), pltpu.SemaphoreType.DMA, pltpu.VMEM((3, 8, 512), i32),
            pltpu.SemaphoreType.DMA((3,)),
        ],
        compiler_params=pltpu.CompilerParams(vmem_limit_bytes=32 << 20),
    )(every, block_slot.reshape(1, -1))


def pack_kernel(slot_ref, slots_ref, cluster_ref, emb_ref, out_ref, ids_ref, raw, sems):
    plane = pl.program_id(0)
    held = out_ref.shape[1]

    @pl.when(plane == 0)
    def _():
        for p in range(NZ):
            def one(n, carry):
                pltpu.make_async_copy(
                    emb_ref.at[:, slot_ref[p, n], :], raw.at[p, n], sems.at[p]
                ).start()
                return carry

            lax.fori_loop(0, held, one, 0, unroll=4)

    hot = lax.broadcasted_iota(jnp.int32, (512, 128), 0) == slots_ref[pl.ds(plane, 1), :]
    ids = jnp.dot(
        cluster_ref[...].astype(jnp.bfloat16), jnp.where(hot, 1.0, 0.0).astype(jnp.bfloat16),
        preferred_element_type=jnp.float32,
    )
    ids_ref[0] = ids.astype(jnp.bfloat16)
    pltpu.make_async_copy(raw.at[plane], raw.at[plane], sems.at[plane]).wait()
    for n in range(0, held, 4):
        rows = raw[plane, n:n + 4]
        scale = lax.rsqrt(jnp.sum(rows * rows, axis=-1, keepdims=True) + jnp.float32(1e-06))
        out_ref[0, n:n + 4] = (rows * scale).astype(jnp.bfloat16)


def pack(embeddings, cluster_ids, slots, slots_smem, held):
    return pl.pallas_call(
        pack_kernel,
        grid=(NZ,),
        in_specs=[
            pl.BlockSpec(memory_space=pltpu.SMEM),
            pl.BlockSpec((NZ, 128), lambda p: (0, 0)),
            pl.BlockSpec((ROWS, 512), lambda p: (0, 0)),
            pl.BlockSpec(memory_space=pl.ANY),
        ],
        out_specs=(
            pl.BlockSpec((1, held, ROWS, 512), lambda p: (p, 0, 0, 0)),
            pl.BlockSpec((1, ROWS, 128), lambda p: (p, 0, 0)),
        ),
        scratch_shapes=[
            pltpu.VMEM((NZ, held, ROWS, 512), jnp.float32),
            pltpu.SemaphoreType.DMA((NZ,)),
        ],
        out_shape=(
            jax.ShapeDtypeStruct((NZ, held, ROWS, 512), jnp.bfloat16),
            jax.ShapeDtypeStruct((NZ, ROWS, 128), jnp.bfloat16),
        ),
        compiler_params=pltpu.CompilerParams(
            dimension_semantics=("arbitrary",), vmem_limit_bytes=32 << 20
        ),
    )(slots_smem, slots, cluster_ids, embeddings)


PIECES = tuple((dz, slice(0, 512)) for dz in (0, 1, 7, 2, 6, 3, 5)) + ((4, slice(0, 256)), (4, slice(256, 512)))
NP = len(PIECES)


def spread_kernel(sel_ref, rows_ref, ids_ref, out_ref, idout_ref, *scratch):
    land = scratch[:NP - 1]
    idland = scratch[NP - 1:NP + 6]
    pick = scratch[NP + 6:2 * NP + 6]
    zsend, zrecv, psend, precv, csend, crecv, isend, irecv, jsend, jrecv, local_sem, bsend, brecv = scratch[2 * NP + 6:]
    x, z, c, y = position()
    greet()

    z_copies = [()]
    for i, (dz, cut) in enumerate(PIECES[1:], 1):
        copies = []
        if cut.start == 0:
            copies.append(send(
                ids_ref.at[(z + dz) % 8], idland[dz - 1], isend.at[dz], irecv.at[dz], (0, 0, dz, 0)
            ))
        copies.append(send(
            rows_ref.at[(z + dz) % 8, :, :, cut], land[i - 1], zsend.at[i], zrecv.at[i], (0, 0, dz, 0)
        ))
        z_copies.append(copies)

    p_copies, l_copies, c_copies = [], [], []

    def plane_send(i):
        dz, cut = PIECES[i]
        for copy in z_copies[i]:
            copy.wait_recv()

        def chip(q, carry):
            for n in range(KCHIP):
                at = sel_ref[n, z * NXY + q]
                pick[i][q, n] = rows_ref[z, at] if i == 0 else land[i - 1][at]
            return carry

        lax.fori_loop(0, NXY, chip, 0)
        id_src = ids_ref.at[z] if i == 0 else idland[dz - 1]
        copies, within = [], []
        for d, (dx, dy) in enumerate(STEPS_XY):
            q = ((x + dx) % 4) * 4 + (y + dy) % 4
            src, dst = pick[i].at[q], out_ref.at[0, :, d, dz, :, cut]
            id_dst = idout_ref.at[0, d, dz]
            if d:
                if cut.start == 0:
                    copies.append(send(id_src, id_dst, jsend.at[dz, d], jrecv.at[dz, d], (dx, dy, 0, 0)))
                copies.append(send(src, dst, psend.at[i, d], precv.at[i, d], (dx, dy, 0, 0)))
                continue
            if cut.start == 0:
                within.append(pltpu.make_async_copy(id_src, id_dst, local_sem.at[i, 1]))
            within.append(pltpu.make_async_copy(src, dst, local_sem.at[i, 0]))
        for copy in within:
            copy.start()
        p_copies.append(copies)
        l_copies.append(within)

    def core_send(i):
        dz, cut = PIECES[i]
        for copy in p_copies[i]:
            copy.wait_recv()
        for copy in l_copies[i]:
            copy.wait()
        copies = [send(
            out_ref.at[0, :, :, dz, :, cut], out_ref.at[1, :, :, dz, :, cut], csend.at[i], crecv.at[i], (0, 0, 0, 1)
        )]
        if cut.start == 0:
            copies.append(send(
                idout_ref.at[0, :, dz], idout_ref.at[1, :, dz], bsend.at[dz], brecv.at[dz], (0, 0, 0, 1)
            ))
        c_copies.append(copies)

    for i in range(NP):
        plane_send(i)
        if i >= 2:
            core_send(i - 2)
    core_send(NP - 2)
    core_send(NP - 1)
    for i in range(NP):
        for copy in c_copies[i]:
            copy.wait()
        for copy in p_copies[i]:
            copy.wait_send()
        for copy in z_copies[i]:
            copy.wait_send()


def spread(sel, rows, ids, collective_id):
    dma = pltpu.SemaphoreType.DMA
    held = rows.shape[1]
    wide = [cut.stop - cut.start for _, cut in PIECES]
    return pl.pallas_call(
        spread_kernel,
        out_shape=(
            jax.ShapeDtypeStruct((NC, KCHIP, NXY, NZ, ROWS, 512), jnp.bfloat16),
            jax.ShapeDtypeStruct((NC, NXY, NZ, ROWS, 128), jnp.bfloat16),
        ),
        in_specs=[
            pl.BlockSpec(memory_space=pltpu.SMEM),
            pl.BlockSpec(memory_space=pltpu.VMEM),
            pl.BlockSpec(memory_space=pltpu.VMEM),
        ],
        out_specs=(pl.BlockSpec(memory_space=pl.ANY), pl.BlockSpec(memory_space=pl.ANY)),
        scratch_shapes=[pltpu.VMEM((held, ROWS, w), jnp.bfloat16) for w in wide[1:]]
        + [pltpu.VMEM((ROWS, 128), jnp.bfloat16)] * 7
        + [pltpu.VMEM((NXY, KCHIP, ROWS, w), jnp.bfloat16) for w in wide]
        + [
            dma((NP,)), dma((NP,)), dma((NP, NXY)), dma((NP, NXY)), dma((NP,)), dma((NP,)),
            dma((NZ,)), dma((NZ,)), dma((NZ, NXY)), dma((NZ, NXY)), dma((NP, 2)), dma((NZ,)), dma((NZ,)),
        ],
        compiler_params=pltpu.CompilerParams(
            collective_id=collective_id, has_side_effects=True, vmem_limit_bytes=48 << 20
        ),
    )(sel, rows, ids)


TILE_I, TILE_J = 256, 512


def maxima_kernel(info_ref, left_ref, right_ref, ids_ref, best_ref, id_col, id_row, col_max):
    e = pl.program_id(0)
    length = 2048

    @pl.when(e == 0)
    def _():
        best_ref[...] = jnp.full((8, length), -1.0, jnp.float32)

    @pl.when(info_ref[e] > 0)
    def _():
        la, lb = info_ref[4 + e], info_ref[8 + e]
        ka, kb = info_ref[12 + e], info_ref[16 + e]
        same = (la == lb).astype(jnp.int32)
        lane = lax.broadcasted_iota(jnp.int32, (length, 128), 1)
        ids = ids_ref[...]
        picked = jnp.where(lane == ka, ids.astype(jnp.float32), 0.0)
        id_col[...] = jnp.sum(picked, axis=1, keepdims=True)
        hot = (lax.broadcasted_iota(jnp.int32, (8, 128), 1) == kb).astype(jnp.bfloat16)
        id_row[...] = lax.dot_general(hot, ids, (((1,), (1,)), ((), ())), preferred_element_type=jnp.float32)
        col_max[...] = jnp.full((8, length), -1.0, jnp.float32)
        for i in range(length // TILE_I):
            half, at = divmod(i * TILE_I, length // 2)
            piece = left_ref[half, 0, at:at + TILE_I, :]
            ida = id_col[i * TILE_I:(i + 1) * TILE_I, :]
            row_max = jnp.full((TILE_I, 128), -1.0, jnp.float32)
            for j in range(length // TILE_J):
                half_j, at_j = divmod(j * TILE_J, length // 2)
                other = right_ref[half_j, 0, at_j:at_j + TILE_J, :]
                gram = lax.dot_general(
                    piece, other, (((1,), (1,)), ((), ())), preferred_element_type=jnp.float32
                )
                keep = ida == id_row[0:1, j * TILE_J:(j + 1) * TILE_J]
                masked = jnp.where(keep, gram, -1.0)
                if i * TILE_I // TILE_J == j:
                    rows = lax.broadcasted_iota(jnp.int32, (TILE_I, TILE_J), 0) + i * TILE_I
                    cols = lax.broadcasted_iota(jnp.int32, (TILE_I, TILE_J), 1) + j * TILE_J
                    masked = jnp.where((rows == cols) & (same == 1), -1.0, masked)
                for g in range(TILE_J // 128):
                    row_max = jnp.maximum(row_max, masked[:, g * 128:(g + 1) * 128])
                span = slice(j * TILE_J, (j + 1) * TILE_J)
                col_max[:, span] = jnp.maximum(
                    col_max[:, span], jnp.max(masked.reshape(TILE_I // 8, 8, TILE_J), axis=0)
                )
            across = jnp.max(jnp.transpose(row_max), axis=0, keepdims=True)
            span = slice(i * TILE_I, (i + 1) * TILE_I)
            best_ref[pl.ds(la, 1), span] = jnp.maximum(best_ref[pl.ds(la, 1), span], across)
        down = jnp.max(col_max[...], axis=0, keepdims=True)
        best_ref[pl.ds(lb, 1), :] = jnp.maximum(best_ref[pl.ds(lb, 1), :], down)


def maxima(info, blocks, ids):
    block = (NC, 1, 1024, 512)
    return pl.pallas_call(
        maxima_kernel,
        grid_spec=pltpu.PrefetchScalarGridSpec(
            num_scalar_prefetch=1,
            grid=(EDGES // NC,),
            in_specs=[
                pl.BlockSpec(block, lambda e, s: (0, s[4 + e], 0, 0)),
                pl.BlockSpec(block, lambda e, s: (0, s[8 + e], 0, 0)),
                pl.BlockSpec((2048, 128), lambda e, s: (0, 0)),
            ],
            out_specs=pl.BlockSpec((8, 2048), lambda e, s: (0, 0)),
            scratch_shapes=[
                pltpu.VMEM((2048, 1), jnp.float32),
                pltpu.VMEM((8, 2048), jnp.float32),
                pltpu.VMEM((8, 2048), jnp.float32),
            ],
        ),
        out_shape=jax.ShapeDtypeStruct((8, 2048), jnp.float32),
        compiler_params=pltpu.CompilerParams(
            dimension_semantics=("arbitrary",), vmem_limit_bytes=60 << 20
        ),
    )(info, blocks, blocks, ids)


def return_kernel(best_ref, out_ref, other, merged, stage, land, table, turned, tiles, csend, crecv, psend, precv, zsend, zrecv):
    x, z, c, y = position()
    greet()
    half = SETS * ROWS
    send(best_ref.at[:, half:], other, csend, crecv, (0, 0, 0, 1)).wait()
    merged[...] = jnp.maximum(best_ref[:, :half], other[...])
    stage[...] = jnp.zeros((NXY, 8, 128), jnp.float32)
    for d in range(NXY):
        stage[d, :, 0:64] = merged[:, d * 64:(d + 1) * 64]
    copies = [
        send(stage.at[d], land.at[d], psend.at[d], precv.at[d], (-dx, -dy, 0, 0))
        for d, (dx, dy) in enumerate(STEPS_XY) if d
    ]
    table[:, x * 4 + y, :] = stage[0]
    for copy in copies:
        copy.wait()
    for d, (dx, dy) in enumerate(STEPS_XY):
        if d:
            table[:, ((x + dx) % 4) * 4 + (y + dy) % 4, :] = land[d]
    turned[...] = jnp.transpose(table[...].reshape(8 * NXY, 128))
    copies = [
        send(turned.at[pl.ds(dz * 8, 8)], tiles.at[dz], zsend.at[dz], zrecv.at[dz], (0, 0, -dz, 0))
        for dz in range(1, NZ)
    ]
    out_ref[z] = turned[0:8, :]
    for copy in copies:
        copy.wait()
    for dz in range(1, NZ):
        out_ref[(z + dz) % 8] = tiles[dz]


def give_back(best, collective_id):
    dma = pltpu.SemaphoreType.DMA
    f32 = jnp.float32
    return pl.pallas_call(
        return_kernel,
        out_shape=jax.ShapeDtypeStruct((NZ, ROWS, 128), f32),
        in_specs=[pl.BlockSpec(memory_space=pltpu.VMEM)],
        out_specs=pl.BlockSpec(memory_space=pltpu.VMEM),
        scratch_shapes=[
            pltpu.VMEM((8, SETS * ROWS), f32), pltpu.VMEM((8, SETS * ROWS), f32), pltpu.VMEM((NXY, 8, 128), f32),
            pltpu.VMEM((NXY, 8, 128), f32), pltpu.VMEM((8, NXY, 128), f32), pltpu.VMEM((128, 128), f32),
            pltpu.VMEM((NZ, ROWS, 128), f32),
            dma, dma, dma((NXY,)), dma((NXY,)), dma((NZ,)), dma((NZ,)),
        ],
        compiler_params=pltpu.CompilerParams(collective_id=collective_id, has_side_effects=True, vmem_limit_bytes=16 << 20),
    )(best)


def combine_kernel(got_ref, entry_ref, out_ref):
    count = out_ref.shape[1]
    out = [jnp.full((8, count), -1.0, jnp.float32) for _ in range(ROWS)]
    column = lax.broadcasted_iota(jnp.int32, (128, count), 1).astype(jnp.float32)
    for z in range(NZ):
        values = jnp.transpose(jnp.concatenate([got_ref[z], jnp.zeros((120, 128), jnp.float32)], axis=0))
        slot = jnp.concatenate(
            [entry_ref[z * NXY:(z + 1) * NXY, 8 + n:9 + n] for n in range(8)], axis=0
        )
        match = slot == column
        for r in range(ROWS):
            best = jnp.where(match, values[:, r:r + 1], -1.0)
            out[r] = jnp.maximum(out[r], jnp.max(best.reshape(16, 8, count), axis=0))
    out_ref[...] = jnp.concatenate([jnp.max(o, axis=0, keepdims=True) for o in out], axis=0)


def combine(got, entry, count):
    return pl.pallas_call(
        combine_kernel,
        out_shape=jax.ShapeDtypeStruct((ROWS, count), jnp.float32),
        in_specs=[pl.BlockSpec(memory_space=pltpu.VMEM)] * 2,
        out_specs=pl.BlockSpec(memory_space=pltpu.VMEM),
        compiler_params=pltpu.CompilerParams(vmem_limit_bytes=16 << 20),
    )(got, entry)


def planned(embeddings, cluster_ids, block_slot, plan, size):
    slots, slots_smem, local, info, entry = plan
    rows, ids = pack(embeddings, cluster_ids, slots, slots_smem, KPLANES[size])
    blocks, block_ids = spread(local, rows, ids, 1 + 2 * size)
    best = maxima(info, blocks.reshape(NC, KCHIP, 1024, 512), block_ids.reshape(2048, 128))
    return combine(give_back(best, 2 + 2 * size), entry, block_slot.shape[0])


def body(embeddings, cluster_ids, block_slot, pairs):
    needed = pairs.reshape(-1)
    *plan, ok = make_plan(gather_pairs(needed), block_slot)

    def choose(k):
        if k == len(KPLANES):
            return any_pairs(embeddings, cluster_ids, block_slot, needed)
        return lax.cond(
            ok[0] == k + 1,
            lambda: planned(embeddings, cluster_ids, block_slot, plan, k),
            lambda: choose(k + 1),
        )

    return choose(0)


def solution(mesh):
    return jax.shard_map(
        body,
        mesh=mesh,
        in_specs=(
            P(("store", "grp"), None, None),
            P(("store", "grp"), None),
            P(),
            P(("store", "grp"), None),
        ),
        out_specs=P(("store", "grp"), None),
        check_vma=False,
    )
```
